32 devices in a mesh: row: 16 (over z, y, core), col: 2 (over x).
Axes of the slice: x: 2, y: 2, z: 4, core: 2. Of those that a mesh axis runs over, the one named last changes fastest.
Arguments:
- homolog_embedding: float32 [128, 128, 256], P(None, 'row'), may hold values from -6 to 6
- pair_features: float32 [128, 128, 128], P('row', 'col'), may hold values from -6 to 6
- first_operand_matrix: float32 [256, 32], replicated, may hold values from -0.375 to 0.375
- second_operand_matrix: float32 [256, 32], replicated, may hold values from -0.375 to 0.375
- outer_output_weight: float32 [1024, 128], replicated, may hold values from -2 to 2
- triangle_input_weight: float32 [128, 512], replicated, may hold values from -0.5 to 0.5
- output_gate_weight: float32 [128, 128], replicated, may hold values from -0.5 to 0.5
- triangle_output_weight: float32 [128, 128], replicated, may hold values from -0.5 to 0.5
Outputs:
- pair_out: float32 [128, 128, 128], P('row', 'col')
The draws below stay inside these ranges and needn't reach their ends.
All inputs are finite; a program needn't handle non-finite values.
Results may differ from the reference program's by a relative error of at most 0.000057.
Values sent between devices are 32-bit elements; how exact they have to be, the bound alone decides.
A program may use at most 64 MiB of HBM per device.

```python
import jax
import jax.numpy as jnp
from jax import lax

HOMOLOG_COUNT = 128
ROSTER_DEPTH = 256
HALF_WIDTH = 32
CZ = 128
CH = 128
RES_ROW = 8
CHAIN_LENGTH = 128


def block_scale(own_key, dims, split, least, largest):
    gain = 1.0
    for axis_at, parts in split:
        draws = jax.random.uniform(jax.random.fold_in(jax.random.fold_in(own_key, 6), axis_at), (parts,), jnp.float32, least / len(split), largest / len(split))
        gain = gain * jnp.repeat(jnp.exp(draws), dims[axis_at] // parts).reshape((-1,) + (1,) * (len(dims) - 1 - axis_at))
    return gain


def bell_draw(own_key, shape, width, limit, pieces=(), kind=jnp.bfloat16):
    gain = block_scale(own_key, shape, pieces, -0.22, 0.18) if pieces else 1.0
    array = jax.random.normal(own_key, shape, jnp.float32) * width * gain
    return jnp.minimum(jnp.maximum(array, -limit), limit).astype(kind)


def setup_inputs(seed: int = 0) -> dict:
    seeds = jax.random.split(jax.random.key(seed), 9)
    homolog_embedding = bell_draw(seeds[0], (HOMOLOG_COUNT, CHAIN_LENGTH, ROSTER_DEPTH), 1.0, 6.0, ((1, 16),), jnp.float32)
    pair_features = bell_draw(seeds[1], (CHAIN_LENGTH, CHAIN_LENGTH, CZ), 1.0, 6.0, ((0, 16), (1, 2)), jnp.float32)
    first_operand_matrix = bell_draw(seeds[2], (ROSTER_DEPTH, HALF_WIDTH), ROSTER_DEPTH ** -0.5, 0.375, (), jnp.float32)
    second_operand_matrix = bell_draw(seeds[3], (ROSTER_DEPTH, HALF_WIDTH), ROSTER_DEPTH ** -0.5, 0.375, (), jnp.float32)
    outer_output_weight = bell_draw(seeds[4], (HALF_WIDTH * HALF_WIDTH, CZ), (HALF_WIDTH * HALF_WIDTH // HOMOLOG_COUNT) ** -0.5, 2.0, (), jnp.float32)
    triangle_input_weight = bell_draw(seeds[5], (CZ, 4 * CH), CZ ** -0.5, 0.5, (), jnp.float32)
    output_gate_weight = bell_draw(seeds[6], (CZ, CZ), CZ ** -0.5, 0.5, (), jnp.float32)
    triangle_output_weight = bell_draw(seeds[7], (CH, CZ), CH ** -0.5, 0.5, (), jnp.float32)
    return {"homolog_embedding": homolog_embedding, "pair_features": pair_features, "first_operand_matrix": first_operand_matrix, "second_operand_matrix": second_operand_matrix, "outer_output_weight": outer_output_weight, "triangle_input_weight": triangle_input_weight, "output_gate_weight": output_gate_weight, "triangle_output_weight": triangle_output_weight}


epsilon = 1e-05
top_precision = lax.Precision.HIGHEST

def apply_layer_norm(values):
    average = lax.optimization_barrier(jnp.mean(values, -1, keepdims=True))
    centred = values - average
    variance = lax.optimization_barrier(jnp.mean(centred * centred, -1, keepdims=True))
    return centred * lax.rsqrt(variance + epsilon)

def reference(homolog_embedding, pair_features, first_operand_matrix, second_operand_matrix, outer_output_weight, triangle_input_weight, output_gate_weight, triangle_output_weight):
    sequence_number = homolog_embedding.shape[0]
    residue_number = homolog_embedding.shape[1]
    row_block_list = RES_ROW
    normalized_input = apply_layer_norm(homolog_embedding)
    left_alignment_proj = jnp.einsum('bxp,pg->bxg', normalized_input, first_operand_matrix, precision=top_precision)
    right_alignment_proj = jnp.einsum('bxp,pg->bxg', normalized_input, second_operand_matrix, precision=top_precision)
    left_factor_blocks = left_alignment_proj.reshape(sequence_number, residue_number // row_block_list, row_block_list, left_alignment_proj.shape[2]).transpose(1, 0, 2, 3)

    def outer_block(left_factor_block):
        outer_product_total = jnp.einsum('emp,eqk->mqpk', left_factor_block, right_alignment_proj, precision=top_precision) / sequence_number
        flattened = outer_product_total.reshape(row_block_list, residue_number, -1)
        return jnp.einsum('ijf,fz->ijz', flattened, outer_output_weight, precision=top_precision)
    update = lax.map(outer_block, left_factor_blocks).reshape(residue_number, residue_number, -1)
    pair_mid = pair_features + update
    normed_pair = apply_layer_norm(pair_mid)
    hidden_width = triangle_output_weight.shape[0]
    projected = jnp.einsum('ijz,zh->ijh', normed_pair, triangle_input_weight, precision=top_precision)
    left_edge = jax.nn.sigmoid(projected[..., hidden_width:2 * hidden_width]) * projected[..., :hidden_width]
    right_edge = jax.nn.sigmoid(projected[..., 3 * hidden_width:]) * projected[..., 2 * hidden_width:3 * hidden_width]
    gate_act = jax.nn.sigmoid(jnp.einsum('ijz,zy->ijy', normed_pair, output_gate_weight, precision=top_precision))
    edge_blocks = left_edge.reshape(residue_number // row_block_list, row_block_list, residue_number, hidden_width)

    def triangle_block(edge_block):
        return jnp.einsum('ikc,jkc->ijc', edge_block, right_edge, precision=top_precision)
    mixed_edges = lax.map(triangle_block, edge_blocks).reshape(residue_number, residue_number, hidden_width)
    return pair_mid + gate_act * jnp.einsum('ijc,cz->ijz', apply_layer_norm(mixed_edges), triangle_output_weight, precision=top_precision)
```

```python
import functools

import jax
import jax.numpy as jnp
from jax import lax
from jax.experimental import pallas as pl
from jax.experimental.pallas import tpu as pltpu
from jax.sharding import PartitionSpec as P

epsilon = 1e-05
MESH = pl.DeviceIdType.MESH
f32 = jnp.float32
bf16 = jnp.bfloat16


def split(x):
    hi = x.astype(bf16)
    lo = (x - hi.astype(f32)).astype(bf16)
    return hi, lo


def dot_nn(a, b):
    return lax.dot_general(a, b, (((1,), (0,)), ((), ())), preferred_element_type=f32)


def dot_nt(a, b):
    return lax.dot_general(a, b, (((1,), (1,)), ((), ())), preferred_element_type=f32)


def layer_norm(values):
    average = jnp.mean(values, -1, keepdims=True)
    centred = values - average
    variance = jnp.mean(centred * centred, -1, keepdims=True)
    return centred * lax.rsqrt(variance + epsilon)


def sigmoid(x):
    return 1.0 / (1.0 + jnp.exp(-x))


def kernel(
    dims,
    msa_ref,
    pair_ref,
    first_ref,
    second_ref,
    outer_ref,
    tri_in_ref,
    gate_w_ref,
    tri_out_ref,
    out_ref,
    nm_ref,
    lt_ref,
    rt_ref,
    rg,
    wp_ref,
    x_ref,
    pm_ref,
    gate_ref,
    redge_ref,
    lall,
    rbuf,
    mst,
    accb,
    a_up,
    a_down,
    a_y,
    a_core,
    a_recv,
    l_sem,
    ring_cw,
    ring_ccw,
    ring_recv,
    m_send,
    m_recv,
):
    S, I, J, R, C, half, channels = dims
    nr = R // C
    Z = R // 4
    zs = nr // 4
    ring = R // 2
    rows = nr * 64

    r = lax.axis_index("row")
    c = lax.axis_index("col")
    core = lax.rem(r, 2)
    y = lax.rem(lax.div(r, 2), 2)
    z = lax.div(r, 4)
    pos = z + y * (ring - 1 - 2 * z)

    def row_at(zz, yy, cc):
        return zz * 4 + yy * 2 + cc

    def ring_row(q):
        q = lax.rem(q, ring)
        yy = lax.div(q, Z)
        zz = q * (1 - yy) + (ring - 1 - q) * yy
        return row_at(zz, yy, core)

    up_row = row_at(lax.rem(z + 1, Z), y, core)
    down_row = row_at(lax.rem(z + Z - 1, Z), y, core)
    y_row = row_at(z, 1 - y, core)
    core_row = row_at(z, y, 1 - core)

    barrier = pltpu.get_barrier_semaphore()
    greet = [(up_row, c), (down_row, c), (y_row, c), (core_row, c)]
    for d in range(1, C):
        other = lax.rem(c + d, C)
        greet += [(r, other), (core_row, other)]
    for target in greet:
        pl.semaphore_signal(barrier, inc=1, device_id=target, device_id_type=MESH)

    both = jnp.concatenate(
        [first_ref[...], second_ref[...], jnp.zeros((first_ref.shape[0], 128 - 2 * half), f32)], 1
    ).T
    both_h, both_l = split(both[: 2 * half])
    both_hl = jnp.concatenate([both_h, both_l], 0)
    depth = msa_ref.shape[1]
    normed = layer_norm(msa_ref[...])
    for n in range(depth // 128):
        nm_ref[n] = normed[:, n * 128 : (n + 1) * 128]
    for m in range(I):
        xh, xl = split(
            jnp.concatenate([nm_ref[n, pl.ds(m, S, stride=I), :] for n in range(depth // 128)], 1)
        )
        t = dot_nt(both_hl, xh)
        t = t[: 2 * half] + t[2 * half :] + dot_nt(both_h, xl)
        lt_ref[m * half : (m + 1) * half, :] = t[:half] * (1.0 / S)
        rt_ref[m * half : (m + 1) * half, :] = t[half:]

    @pl.when(lax.div(r, nr) == c)
    def _():
        slot = lax.rem(r, nr)
        for b in range(half):
            rg[slot, b * I : (b + 1) * I, :] = rt_ref[pl.ds(b, I, stride=half), :]

    pl.semaphore_wait(barrier, len(greet))

    def a_copy(slot, send, target):
        return pltpu.make_async_remote_copy(
            src_ref=rg.at[slot],
            dst_ref=rg.at[slot],
            send_sem=send,
            recv_sem=a_recv.at[slot],
            device_id=(target, c),
            device_id_type=MESH,
        )

    flip = (z > c * zs).astype(jnp.int32)

    def near(t):
        return t + flip * (zs - 1 - 2 * t)

    def a_links(t):
        zi = near(t)
        source = c * zs + zi
        slot = zi * 4 + y * 2 + core
        return (
            slot,
            source,
            jnp.logical_and(z >= source, z < Z - 1),
            jnp.logical_and(z <= source, z > 0),
        )

    for t in range(zs):
        slot, source, goes_up, goes_down = a_links(t)

        @pl.when(z != source)
        def _():
            a_copy(slot, a_y.at[t], y_row).wait_recv()

        @pl.when(goes_up)
        def _():
            a_copy(slot, a_up.at[t], up_row).start()

        @pl.when(goes_down)
        def _():
            a_copy(slot, a_down.at[t], down_row).start()

        a_copy(slot, a_y.at[t], y_row).start()
        a_copy(slot, a_core.at[t, 0], core_row).start()

    for b in range(half):
        wp_ref[b * half : (b + 1) * half, :] = outer_ref[pl.ds(b, half, stride=half), :]

    lt = lt_ref[...]
    lt_h, lt_l = split(lt)
    lt_hh = jnp.concatenate([lt_h, lt_h], 1)
    lane = lax.broadcasted_iota(jnp.int32, (half // 4, I, 128), 2)
    low64 = lane < 64
    low32 = lax.rem(lane, 64) < 32

    def outer_block(slot):
        rh, rl = split(rg[slot])
        o = dot_nt(jnp.concatenate([rh, rl], 1), lt_hh) + dot_nt(rh, lt_l)
        o = o.reshape(half // 4, 4, I, half * I)
        for h in range(half * I // 128):
            x = [o[:, q, :, h * 128 : (h + 1) * 128] for q in range(4)]
            w = [None] * 4
            for q in range(2):
                w[q] = jnp.where(low64, x[q], pltpu.roll(x[q + 2], 64, 2))
                w[q + 2] = jnp.where(low64, pltpu.roll(x[q], 64, 2), x[q + 2])
            v = [None] * 4
            for q in (0, 2):
                v[q] = jnp.where(low32, w[q], pltpu.roll(w[q + 1], 32, 2))
                v[q + 1] = jnp.where(low32, pltpu.roll(w[q], 96, 2), w[q + 1])
            for q in range(4):
                i = h * 4 + q
                for g in range(half // 4):
                    x_ref[slot, i * I : (i + 1) * I, g * 128 : (g + 1) * 128] = v[q][g]

    for t in range(zs):
        slot = a_links(t)[0]
        outer_block(slot)
    for t in range(zs):
        slot = near(t) * 4 + (1 - y) * 2 + core
        a_copy(slot, a_core.at[t, 1], core_row).wait_recv()
        a_copy(slot, a_core.at[t, 1], core_row).start()
    for t in range(zs):
        outer_block(near(t) * 4 + (1 - y) * 2 + core)
    for yy in range(2):
        for t in range(zs):
            slot = near(t) * 4 + lax.rem(y + yy, 2) * 2 + 1 - core
            a_copy(slot, a_core.at[t, 1], core_row).wait_recv()
            outer_block(slot)

    wh, wl = split(wp_ref[...])
    w_hl = jnp.concatenate([wh, wl], 1)
    in_w = jnp.concatenate([tri_in_ref[...], gate_w_ref[...]], 1)
    in_h, in_l = split(in_w)
    in_hh = jnp.concatenate([in_h, in_h], 0)
    chunk_slots = min(4, nr)
    chunk = chunk_slots * 64
    for n in range(nr // chunk_slots):
        xh, xl = split(x_ref[n * chunk_slots : (n + 1) * chunk_slots].reshape(chunk, half * half))
        t = dot_nn(xh, w_hl)
        t = t[:, :channels] + t[:, channels:] + dot_nn(xl, wh)
        own = jnp.concatenate(
            [
                pair_ref[i * J + s * I : i * J + (s + 1) * I, :]
                for s in range(n * chunk_slots, (n + 1) * chunk_slots)
                for i in range(I)
            ],
            0,
        )
        mid = own + t
        sl = pl.ds(n * chunk, chunk)
        pm_ref[sl, :] = mid
        nh, nl = split(layer_norm(mid))
        pr = dot_nn(jnp.concatenate([nh, nl], 1), in_hh) + dot_nn(nh, in_l)
        ch = tri_out_ref.shape[0]
        lall[core, sl, :] = sigmoid(pr[:, ch : 2 * ch]) * pr[:, :ch]
        redge_ref[sl, :] = sigmoid(pr[:, 3 * ch : 4 * ch]) * pr[:, 2 * ch : 3 * ch]
        gate_ref[sl, :] = sigmoid(pr[:, 4 * ch :])

    for s in range(nr):
        for k in range(I):
            at = (s * I + k) * I
            rbuf[0, at : at + I, :] = redge_ref[pl.ds(s * 64 + k, I, stride=I), :]

    part = rows // 2

    def ring_copy(src, dst, h, send, target):
        return pltpu.make_async_remote_copy(
            src_ref=rbuf.at[src, pl.ds(h * part, part)],
            dst_ref=rbuf.at[dst, pl.ds(h * part, part)],
            send_sem=send,
            recv_sem=ring_recv.at[dst, h],
            device_id=(target, c),
            device_id_type=MESH,
        )

    next_row = ring_row(pos + 1)
    prev_row = ring_row(pos + ring - 1)
    far = ring // 2

    def cw(t, h):
        return ring_copy(t, t + 1, h, ring_cw.at[t, h], next_row)

    def ccw(t, h):
        return ring_copy((ring - t) % ring, ring - t - 1, h, ring_ccw.at[t, h], prev_row)

    l_copy = pltpu.make_async_remote_copy(
        src_ref=lall.at[core],
        dst_ref=lall.at[core],
        send_sem=l_sem.at[0],
        recv_sem=l_sem.at[1],
        device_id=(core_row, c),
        device_id_type=MESH,
    )

    def forward(t):
        for h in range(2):
            if t > 0:
                cw(t - 1, h).wait_recv()
            if t < far - 1 or h == 0:
                cw(t, h).start()
            if t > 0:
                ccw(t - 1, h).wait_recv()
            if t < far - 1 or h == 1:
                ccw(t, h).start()

    def piece(d, q):
        source = ring_row(pos + ring - d)
        dest_col = lax.div(source, nr)
        target = row_at(z, y, lax.rem(core + q, 2))
        return (
            dest_col,
            lax.rem(source, nr),
            pltpu.make_async_remote_copy(
                src_ref=mst.at[d, q],
                dst_ref=accb.at[c, lax.rem(source, nr)],
                send_sem=m_send.at[d, q],
                recv_sem=m_recv.at[c, lax.rem(source, nr)],
                device_id=(target, dest_col),
                device_id_type=MESH,
            ),
        )

    def triangle(blocks):
        for q in (1, 0):
            who = lax.rem(core + q, 2)

            def step(s, acc):
                acc = list(acc)
                for k in range(I):
                    rv = [rbuf[d, pl.ds(pl.multiple_of((s * I + k) * I, I), I), :] for d in blocks]
                    for i in range(I):
                        lv = lall[who, pl.ds(s * 64 + i * I + k, 1), :]
                        for n in range(len(blocks)):
                            acc[n * I + i] = acc[n * I + i] + lv * rv[n]
                return tuple(acc)

            acc = lax.fori_loop(
                0, nr, step, tuple(jnp.zeros((I, channels), f32) for _ in range(I * len(blocks)))
            )
            for n, d in enumerate(blocks):
                for i in range(I):
                    mst[d, q, i * I : (i + 1) * I, :] = acc[n * I + i]
                dest_col, slot, copy = piece(d, q)
                if q == 1:
                    copy.start()
                else:

                    @pl.when(dest_col == c)
                    def _():
                        accb[c, slot] = mst[d, q]

                    @pl.when(dest_col != c)
                    def _():
                        copy.start()

    forward(0)
    l_copy.start()
    l_copy.wait_recv()
    triangle([0])
    for t in range(1, far):
        forward(t)
        triangle([t, ring - t])
    cw(far - 1, 0).wait_recv()
    ccw(far - 1, 1).wait_recv()
    triangle([far])

    for s in range(nr):
        for k in range(C):
            mine = jnp.logical_and(c == k, core == s % 2)

            @pl.when(jnp.logical_not(mine))
            def _():
                pltpu.make_async_remote_copy(
                    src_ref=mst.at[0, 0],
                    dst_ref=accb.at[k, s],
                    send_sem=m_send.at[0, 0],
                    recv_sem=m_recv.at[k, s],
                    device_id=(core_row, c),
                    device_id_type=MESH,
                ).wait_recv()

    out_h, out_l = split(tri_out_ref[...])
    out_hh = jnp.concatenate([out_h, out_h], 0)
    for n in range(nr // chunk_slots):
        sl = pl.ds(n * chunk, chunk)
        mixed = accb[0, n * chunk_slots : (n + 1) * chunk_slots].reshape(chunk, channels)
        for k in range(1, C):
            mixed = mixed + accb[k, n * chunk_slots : (n + 1) * chunk_slots].reshape(chunk, channels)
        nh, nl = split(layer_norm(mixed))
        t = dot_nn(jnp.concatenate([nh, nl], 1), out_hh) + dot_nn(nh, out_l)
        t = pm_ref[sl, :] + gate_ref[sl, :] * t
        for s in range(chunk_slots):
            for i in range(I):
                at = i * J + (n * chunk_slots + s) * I
                out_ref[at : at + I, :] = t[(s * I + i) * I : (s * I + i + 1) * I]

    for t in range(zs):
        slot, source, goes_up, goes_down = a_links(t)

        @pl.when(goes_up)
        def _():
            a_copy(slot, a_up.at[t], up_row).wait_send()

        @pl.when(goes_down)
        def _():
            a_copy(slot, a_down.at[t], down_row).wait_send()

        a_copy(slot, a_y.at[t], y_row).wait_send()
        a_copy(slot, a_core.at[t, 0], core_row).wait_send()
        a_copy(near(t) * 4 + (1 - y) * 2 + core, a_core.at[t, 1], core_row).wait_send()
    l_copy.wait_send()
    for t in range(far):
        for h in range(2):
            if t < far - 1 or h == 0:
                cw(t, h).wait_send()
            if t < far - 1 or h == 1:
                ccw(t, h).wait_send()
    for d in range(ring):
        dest_col, _, copy = piece(d, 0)

        @pl.when(dest_col != c)
        def _():
            copy.wait_send()

        piece(d, 1)[2].wait_send()


def per_device(R, C, msa, pair, first, second, outer_w, tri_in, gate_w, tri_out):
    S, I, depth = msa.shape
    J, channels = pair.shape[1:]
    half = first.shape[1]
    nr = R // C
    zs = nr // 4
    ring = R // 2
    rows = nr * I * I
    dma = pltpu.SemaphoreType.DMA
    out = pl.pallas_call(
        functools.partial(kernel, (S, I, J, R, C, half, channels)),
        out_shape=jax.ShapeDtypeStruct((I * J, channels), f32),
        in_specs=[pl.BlockSpec(memory_space=pltpu.VMEM)] * 8,
        out_specs=pl.BlockSpec(memory_space=pltpu.VMEM),
        scratch_shapes=[
            pltpu.VMEM((depth // 128, S * I, 128), f32),
            pltpu.VMEM((I * half, S), f32),
            pltpu.VMEM((I * half, S), f32),
            pltpu.VMEM((nr, half * I, S), f32),
            pltpu.VMEM((half * half, channels), f32),
            pltpu.VMEM((nr, I * I, half * half), f32),
            pltpu.VMEM((rows, channels), f32),
            pltpu.VMEM((rows, channels), f32),
            pltpu.VMEM((rows, channels), f32),
            pltpu.VMEM((2, rows, channels), f32),
            pltpu.VMEM((ring, rows, channels), f32),
            pltpu.VMEM((ring, 2, I * I, channels), f32),
            pltpu.VMEM((C, nr, I * I, channels), f32),
            dma((zs,)),
            dma((zs,)),
            dma((zs,)),
            dma((zs, 2)),
            dma((nr,)),
            dma((2,)),
            dma((ring // 2, 2)),
            dma((ring // 2, 2)),
            dma((ring, 2)),
            dma((ring, 2)),
            dma((C, nr)),
        ],
        compiler_params=pltpu.CompilerParams(
            collective_id=0, has_side_effects=True, vmem_limit_bytes=48 * 1024 * 1024
        ),
        cost_estimate=pl.CostEstimate(
            flops=6 * 180 * 10**6, bytes_accessed=3 * 10**6, transcendentals=200000
        ),
    )(
        msa.reshape(S * I, depth),
        pair.reshape(I * J, channels),
        first,
        second,
        outer_w,
        tri_in,
        gate_w,
        tri_out,
    )
    return out.reshape(I, J, channels)


def solution(mesh):
    placed = (P(None, "row", None), P("row", "col", None), P(), P(), P(), P(), P(), P())
    return jax.shard_map(
        functools.partial(per_device, mesh.shape["row"], mesh.shape["col"]),
        mesh=mesh,
        in_specs=placed,
        out_specs=P("row", "col", None),
        check_vma=False,
    )
```

```python
import functools

import jax
import jax.numpy as jnp
from jax import lax
from jax.experimental import pallas as pl
from jax.experimental.pallas import tpu as pltpu
from jax.sharding import PartitionSpec as P

epsilon = 1e-05
MESH = pl.DeviceIdType.MESH
f32 = jnp.float32
bf16 = jnp.bfloat16
pieces = 4


def split(x):
    hi = x.astype(bf16)
    lo = (x - hi.astype(f32)).astype(bf16)
    return hi, lo


def dot_nn(a, b):
    return lax.dot_general(a, b, (((1,), (0,)), ((), ())), preferred_element_type=f32)


def dot_nt(a, b):
    return lax.dot_general(a, b, (((1,), (1,)), ((), ())), preferred_element_type=f32)


def layer_norm(values):
    average = jnp.mean(values, -1, keepdims=True)
    centred = values - average
    variance = jnp.mean(centred * centred, -1, keepdims=True)
    return centred * lax.rsqrt(variance + epsilon)


def sigmoid(x):
    return 1.0 / (1.0 + jnp.exp(-x))


def kernel(
    dims,
    msa_hbm,
    pair_hbm,
    first_hbm,
    second_hbm,
    outer_hbm,
    tri_in_hbm,
    gate_w_hbm,
    tri_out_hbm,
    out_ref,
    msa_ref,
    pair_ref,
    first_ref,
    second_ref,
    outer_ref,
    tri_in_ref,
    gate_w_ref,
    tri_out_ref,
    nm_ref,
    lt_ref,
    rt_ref,
    rg,
    wp_ref,
    x_ref,
    pm_ref,
    gate_ref,
    redge_ref,
    lall,
    rbuf,
    mst,
    accb,
    a_up,
    a_down,
    a_y,
    a_core,
    a_recv,
    in_sem,
    l_sem,
    ring_cw,
    ring_ccw,
    ring_recv,
    m_send,
    m_recv,
):
    S, I, J, R, C, half, channels = dims
    nr = R // C
    Z = R // 4
    zs = nr // 4
    ring = R // 2
    rows = nr * 64
    parts = max(2, zs)

    r = lax.axis_index("row")
    c = lax.axis_index("col")
    core = lax.rem(r, 2)
    y = lax.rem(lax.div(r, 2), 2)
    z = lax.div(r, 4)
    pos = z + y * (ring - 1 - 2 * z)

    def row_at(zz, yy, cc):
        return zz * 4 + yy * 2 + cc

    def ring_row(q):
        q = lax.rem(q, ring)
        yy = lax.div(q, Z)
        zz = q * (1 - yy) + (ring - 1 - q) * yy
        return row_at(zz, yy, core)

    up_row = row_at(lax.rem(z + 1, Z), y, core)
    down_row = row_at(lax.rem(z + Z - 1, Z), y, core)
    y_row = row_at(z, 1 - y, core)
    core_row = row_at(z, y, 1 - core)

    loads = [
        pltpu.make_async_copy(src, dst, in_sem.at[n])
        for n, (src, dst) in enumerate(
            (
                (msa_hbm, msa_ref),
                (first_hbm, first_ref),
                (second_hbm, second_ref),
                (outer_hbm, outer_ref),
                (pair_hbm, pair_ref),
                (tri_in_hbm, tri_in_ref),
                (gate_w_hbm, gate_w_ref),
                (tri_out_hbm, tri_out_ref),
            )
        )
    ]
    for load in loads:
        load.start()

    barrier = pltpu.get_barrier_semaphore()
    greet = [(up_row, c), (down_row, c), (y_row, c), (core_row, c)]
    for d in range(1, C):
        other = lax.rem(c + d, C)
        greet += [(r, other), (core_row, other)]
    for target in greet:
        pl.semaphore_signal(barrier, inc=1, device_id=target, device_id_type=MESH)

    for load in loads[:3]:
        load.wait()
    both = jnp.concatenate([first_ref[...], second_ref[...]], 0)
    both_h, both_l = split(both)
    both_hl = jnp.concatenate([both_h, both_l], 0)
    depth = msa_ref.shape[1]
    normed = layer_norm(msa_ref[...])
    for n in range(depth // 128):
        nm_ref[n] = normed[:, n * 128 : (n + 1) * 128]
    for m in range(I):
        xh, xl = split(
            jnp.concatenate([nm_ref[n, pl.ds(m, S, stride=I), :] for n in range(depth // 128)], 1)
        )
        t = dot_nt(both_hl, xh)
        t = t[: 2 * half] + t[2 * half :] + dot_nt(both_h, xl)
        lt_ref[m * half : (m + 1) * half, :] = t[:half] * (1.0 / S)
        rt_ref[m * half : (m + 1) * half, :] = t[half:]

    @pl.when(lax.div(r, nr) == c)
    def _():
        slot = lax.rem(r, nr)
        for b in range(half):
            rg[slot, b * I : (b + 1) * I, :] = rt_ref[pl.ds(b, I, stride=half), :]

    pl.semaphore_wait(barrier, len(greet))

    piece_rows = half * I // pieces

    def a_copy(slot, u, send, target):
        at = rg.at[slot, pl.ds(u * piece_rows, piece_rows)]
        return pltpu.make_async_remote_copy(
            src_ref=at,
            dst_ref=at,
            send_sem=send,
            recv_sem=a_recv.at[slot, u],
            device_id=(target, c),
            device_id_type=MESH,
        )

    def turned(t, zz):
        flip = (zz > c * zs).astype(jnp.int32)
        return t + flip * (zs - 1 - 2 * t)

    def a_links(t):
        zi = turned(t, z)
        source = c * zs + zi
        slot = zi * 4 + y * 2 + core
        return (
            slot,
            source,
            jnp.logical_and(z >= source, z < Z - 1),
            jnp.logical_and(z <= source, z > 0),
        )

    def a_line(t):
        slot, source, goes_up, goes_down = a_links(t)
        for u in range(pieces):

            @pl.when(z != source)
            def _():
                a_copy(slot, u, a_y.at[t, u], y_row).wait_recv()

            @pl.when(goes_up)
            def _():
                a_copy(slot, u, a_up.at[t, u], up_row).start()

            @pl.when(goes_down)
            def _():
                a_copy(slot, u, a_down.at[t, u], down_row).start()

            a_copy(slot, u, a_y.at[t, u], y_row).start()
            a_copy(slot, u, a_core.at[t, 0, u], core_row).start()

    def a_across(t):
        slot = turned(t, z) * 4 + (1 - y) * 2 + core
        for u in range(pieces):
            a_copy(slot, u, a_core.at[t, 1, u], core_row).wait_recv()
            a_copy(slot, u, a_core.at[t, 1, u], core_row).start()

    a_line(0)

    loads[3].wait()
    for b in range(half):
        wp_ref[b * half : (b + 1) * half, :] = outer_ref[pl.ds(b, half, stride=half), :]

    lt = lt_ref[...]
    lt_h, lt_l = split(lt)
    lt_hh = jnp.concatenate([lt_h, lt_h], 1)
    lane = lax.broadcasted_iota(jnp.int32, (half // 4, I, 128), 2)
    low64 = lane < 64
    low32 = lax.rem(lane, 64) < 32

    def outer_block(slot):
        rh, rl = split(rg[slot])
        o = dot_nt(jnp.concatenate([rh, rl], 1), lt_hh) + dot_nt(rh, lt_l)
        o = o.reshape(half // 4, 4, I, half * I)
        for h in range(half * I // 128):
            x = [o[:, q, :, h * 128 : (h + 1) * 128] for q in range(4)]
            w = [None] * 4
            for q in range(2):
                w[q] = jnp.where(low64, x[q], pltpu.roll(x[q + 2], 64, 2))
                w[q + 2] = jnp.where(low64, pltpu.roll(x[q], 64, 2), x[q + 2])
            v = [None] * 4
            for q in (0, 2):
                v[q] = jnp.where(low32, w[q], pltpu.roll(w[q + 1], 32, 2))
                v[q + 1] = jnp.where(low32, pltpu.roll(w[q], 96, 2), w[q + 1])
            for q in range(4):
                i = h * 4 + q
                for g in range(half // 4):
                    x_ref[slot, i * I : (i + 1) * I, g * 128 : (g + 1) * 128] = v[q][g]

    wh, wl = split(wp_ref[...])
    w_hl = jnp.concatenate([wh, wl], 1)
    for load in loads[4:]:
        load.wait()
    in_w = jnp.concatenate([tri_in_ref[...], gate_w_ref[...]], 1)
    in_h, in_l = split(in_w)
    in_hh = jnp.concatenate([in_h, in_h], 0)
    out_h, out_l = split(tri_out_ref[...])
    out_hh = jnp.concatenate([out_h, out_h], 0)
    ch = tri_out_ref.shape[0]
    group = 4 * 64

    def pair_group(zi):
        xh, xl = split(x_ref[pl.ds(zi * 4, 4)].reshape(group, half * half))
        t = dot_nn(xh, w_hl)
        t = t[:, :channels] + t[:, channels:] + dot_nn(xl, wh)
        own = jnp.concatenate(
            [
                pair_ref[pl.ds(pl.multiple_of(i * J + (zi * 4 + s) * I, I), I), :]
                for s in range(4)
                for i in range(I)
            ],
            0,
        )
        mid = own + t
        sl = pl.ds(pl.multiple_of(zi * group, group), group)
        pm_ref[sl, :] = mid
        nh, nl = split(layer_norm(mid))
        pr = dot_nn(jnp.concatenate([nh, nl], 1), in_hh) + dot_nn(nh, in_l)
        redge_ref[sl, :] = sigmoid(pr[:, 3 * ch : 4 * ch]) * pr[:, 2 * ch : 3 * ch]
        for s in range(4):
            for k in range(I):
                at = pl.multiple_of(zi * group + (s * I + k) * I, I)
                rbuf[0, pl.ds(at, I), :] = redge_ref[
                    pl.ds(zi * group + s * 64 + k, I, stride=I), :
                ]
        for n in range(parts // zs):
            h = zi * (parts // zs) + n
            cw(0, h).start()
            ccw(0, h).start()
        lall[core, sl, :] = sigmoid(pr[:, ch : 2 * ch]) * pr[:, :ch]
        l_copy(zi).start()
        gate_ref[sl, :] = sigmoid(pr[:, 4 * ch :])

    part = rows // parts
    next_row = ring_row(pos + 1)
    prev_row = ring_row(pos + ring - 1)
    far = ring // 2

    def ring_copy(src, dst, h, send, target):
        at = pl.ds(pl.multiple_of(h * part, part), part)
        return pltpu.make_async_remote_copy(
            src_ref=rbuf.at[src, at],
            dst_ref=rbuf.at[dst, at],
            send_sem=send,
            recv_sem=ring_recv.at[dst, h],
            device_id=(target, c),
            device_id_type=MESH,
        )

    def cw(t, h):
        return ring_copy(t, t + 1, h, ring_cw.at[t, h], next_row)

    def ccw(t, h):
        return ring_copy((ring - t) % ring, ring - t - 1, h, ring_ccw.at[t, h], prev_row)

    def l_copy(zi):
        at = lall.at[core, pl.ds(pl.multiple_of(zi * group, group), group)]
        return pltpu.make_async_remote_copy(
            src_ref=at,
            dst_ref=at,
            send_sem=l_sem.at[0, zi],
            recv_sem=l_sem.at[1, zi],
            device_id=(core_row, c),
            device_id_type=MESH,
        )

    def block_order(d, h):
        if zs == 1:
            return h
        return turned(h, lax.div(ring_row(pos + ring - d), 4))

    def forward(t):
        if t == far - 1:
            for h in range(parts // 2):
                cw(t - 1, h).wait_recv()
                cw(t, h).start()
                ccw(t - 1, parts // 2 + h).wait_recv()
                ccw(t, parts // 2 + h).start()
            for h in range(parts // 2):
                cw(t - 1, parts // 2 + h).wait_recv()
                ccw(t - 1, h).wait_recv()
            return
        for n in range(parts):
            h = block_order(t, n)
            cw(t - 1, h).wait_recv()
            cw(t, h).start()
            h = block_order(ring - t, n)
            ccw(t - 1, h).wait_recv()
            ccw(t, h).start()

    def piece(d, q):
        source = ring_row(pos + ring - d)
        dest_col = lax.div(source, nr)
        target = row_at(z, y, lax.rem(core + q, 2))
        return (
            dest_col,
            lax.rem(source, nr),
            pltpu.make_async_remote_copy(
                src_ref=mst.at[d, q],
                dst_ref=accb.at[c, lax.rem(source, nr)],
                send_sem=m_send.at[d, q],
                recv_sem=m_recv.at[c, lax.rem(source, nr)],
                device_id=(target, dest_col),
                device_id_type=MESH,
            ),
        )

    def triangle(blocks):
        for q in (1, 0):
            who = lax.rem(core + q, 2)

            def step(s, acc):
                acc = list(acc)
                for k in range(I):
                    rv = [rbuf[d, pl.ds(pl.multiple_of((s * I + k) * I, I), I), :] for d in blocks]
                    for i in range(I):
                        lv = lall[who, pl.ds(s * 64 + i * I + k, 1), :]
                        for n in range(len(blocks)):
                            acc[n * I + i] = acc[n * I + i] + lv * rv[n]
                return tuple(acc)

            acc = lax.fori_loop(
                0, nr, step, tuple(jnp.zeros((I, channels), f32) for _ in range(I * len(blocks)))
            )
            for n, d in enumerate(blocks):
                for i in range(I):
                    mst[d, q, i * I : (i + 1) * I, :] = acc[n * I + i]
                dest_col, slot, copy = piece(d, q)
                if q == 1:
                    copy.start()
                else:

                    @pl.when(dest_col == c)
                    def _():
                        accb[c, slot] = mst[d, q]

                    @pl.when(dest_col != c)
                    def _():
                        copy.start()

    def finish(d):
        source = ring_row(pos + ring - d) - core

        @pl.when(lax.div(source, nr) == c)
        def _():
            base = lax.rem(source, nr)

            def arrived(k, s):
                pltpu.make_async_remote_copy(
                    src_ref=mst.at[0, 0],
                    dst_ref=accb.at[k, s],
                    send_sem=m_send.at[0, 0],
                    recv_sem=m_recv.at[k, s],
                    device_id=(core_row, c),
                    device_id_type=MESH,
                ).wait_recv()

            arrived(c, base + 1 - core)
            for n in range(1, C):
                k = lax.rem(c + n, C)
                arrived(k, base)
                arrived(k, base + 1)
            mixed = accb[0, pl.ds(base, 2)].reshape(128, channels)
            for k in range(1, C):
                mixed = mixed + accb[k, pl.ds(base, 2)].reshape(128, channels)
            nh, nl = split(layer_norm(mixed))
            t = dot_nn(jnp.concatenate([nh, nl], 1), out_hh) + dot_nn(nh, out_l)
            sl = pl.ds(pl.multiple_of(base * 64, 64), 128)
            t = pm_ref[sl, :] + gate_ref[sl, :] * t
            for s in range(2):
                for i in range(I):
                    at = pl.multiple_of(i * J + (base + s) * I, I)
                    out_ref[pl.ds(at, I), :] = t[(s * I + i) * I : (s * I + i + 1) * I]

    outer_block(a_links(0)[0])
    for t in range(1, zs):
        a_line(t)
    a_across(0)
    for t in range(zs):
        zi = turned(t, z)
        if t > 0:
            outer_block(zi * 4 + y * 2 + core)
        outer_block(zi * 4 + (1 - y) * 2 + core)
        for yy in (y, 1 - y):
            slot = zi * 4 + yy * 2 + 1 - core
            for u in range(pieces):
                a_copy(slot, u, a_core.at[t, 1, u], core_row).wait_recv()
            outer_block(slot)
        if t + 1 < zs:
            a_across(t + 1)
        pair_group(zi)

    for t in range(zs):
        l_copy(t).wait_recv()
    pending = [0]
    triangle([0])
    for t in range(1, far):
        forward(t)
        triangle([t, ring - t])
        for d in pending:
            finish(d)
        pending = [t, ring - t]
    for d in pending:
        finish(d)
    for h in range(parts // 2):
        cw(far - 1, h).wait_recv()
        ccw(far - 1, parts // 2 + h).wait_recv()
    triangle([far])
    finish(far)

    for t in range(zs):
        slot, source, goes_up, goes_down = a_links(t)
        across = turned(t, z) * 4 + (1 - y) * 2 + core
        for u in range(pieces):

            @pl.when(goes_up)
            def _():
                a_copy(slot, u, a_up.at[t, u], up_row).wait_send()

            @pl.when(goes_down)
            def _():
                a_copy(slot, u, a_down.at[t, u], down_row).wait_send()

            a_copy(slot, u, a_y.at[t, u], y_row).wait_send()
            a_copy(slot, u, a_core.at[t, 0, u], core_row).wait_send()
            a_copy(across, u, a_core.at[t, 1, u], core_row).wait_send()
        l_copy(t).wait_send()
    for t in range(far):
        for h in range(parts):
            if t < far - 1 or h < parts // 2:
                cw(t, h).wait_send()
            if t < far - 1 or h >= parts // 2:
                ccw(t, h).wait_send()
    for d in range(ring):
        dest_col, _, copy = piece(d, 0)

        @pl.when(dest_col != c)
        def _():
            copy.wait_send()

        piece(d, 1)[2].wait_send()


def per_device(R, C, msa, pair, first, second, outer_w, tri_in, gate_w, tri_out):
    S, I, depth = msa.shape
    J, channels = pair.shape[1:]
    half = first.shape[1]
    nr = R // C
    zs = nr // 4
    ring = R // 2
    rows = nr * I * I
    parts = max(2, zs)
    operands = (
        msa.reshape(S * I, depth),
        pair.reshape(I * J, channels),
        first.T,
        second.T,
        outer_w,
        tri_in,
        gate_w,
        tri_out,
    )
    dma = pltpu.SemaphoreType.DMA
    out = pl.pallas_call(
        functools.partial(kernel, (S, I, J, R, C, half, channels)),
        out_shape=jax.ShapeDtypeStruct((I * J, channels), f32),
        in_specs=[pl.BlockSpec(memory_space=pltpu.HBM)] * 8,
        out_specs=pl.BlockSpec(memory_space=pltpu.VMEM),
        scratch_shapes=[pltpu.VMEM(x.shape, f32) for x in operands]
        + [
            pltpu.VMEM((depth // 128, S * I, 128), f32),
            pltpu.VMEM((I * half, S), f32),
            pltpu.VMEM((I * half, S), f32),
            pltpu.VMEM((nr, half * I, S), f32),
            pltpu.VMEM((half * half, channels), f32),
            pltpu.VMEM((nr, I * I, half * half), f32),
            pltpu.VMEM((rows, channels), f32),
            pltpu.VMEM((rows, channels), f32),
            pltpu.VMEM((rows, channels), f32),
            pltpu.VMEM((2, rows, channels), f32),
            pltpu.VMEM((ring, rows, channels), f32),
            pltpu.VMEM((ring, 2, I * I, channels), f32),
            pltpu.VMEM((C, nr, I * I, channels), f32),
            dma((zs, pieces)),
            dma((zs, pieces)),
            dma((zs, pieces)),
            dma((zs, 2, pieces)),
            dma((nr, pieces)),
            dma((len(operands),)),
            dma((2, zs)),
            dma((ring // 2, parts)),
            dma((ring // 2, parts)),
            dma((ring, parts)),
            dma((ring, 2)),
            dma((C, nr)),
        ],
        compiler_params=pltpu.CompilerParams(
            collective_id=0, has_side_effects=True, vmem_limit_bytes=62 * 1024 * 1024
        ),
        cost_estimate=pl.CostEstimate(
            flops=6 * 180 * 10**6, bytes_accessed=3 * 10**6, transcendentals=200000
        ),
    )(*operands)
    return out.reshape(I, J, channels)


def solution(mesh):
    placed = (P(None, "row", None), P("row", "col", None), P(), P(), P(), P(), P(), P())
    return jax.shard_map(
        functools.partial(per_device, mesh.shape["row"], mesh.shape["col"]),
        mesh=mesh,
        in_specs=placed,
        out_specs=P("row", "col", None),
        check_vma=False,
    )
```

```python
import functools

import jax
import jax.numpy as jnp
from jax import lax
from jax.experimental import pallas as pl
from jax.experimental.pallas import tpu as pltpu
from jax.sharding import PartitionSpec as P

epsilon = 1e-05
MESH = pl.DeviceIdType.MESH
f32 = jnp.float32
bf16 = jnp.bfloat16
pieces = 4


def split(x):
    hi = x.astype(bf16)
    lo = (x - hi.astype(f32)).astype(bf16)
    return hi, lo


def dot_nn(a, b):
    return lax.dot_general(a, b, (((1,), (0,)), ((), ())), preferred_element_type=f32)


def dot_nt(a, b):
    return lax.dot_general(a, b, (((1,), (1,)), ((), ())), preferred_element_type=f32)


def layer_norm(values):
    average = jnp.mean(values, -1, keepdims=True)
    centred = values - average
    variance = jnp.mean(centred * centred, -1, keepdims=True)
    return centred * lax.rsqrt(variance + epsilon)


def sigmoid(x):
    return 1.0 / (1.0 + jnp.exp(-x))


def kernel(
    dims,
    msa_hbm,
    pair_hbm,
    first_hbm,
    second_hbm,
    outer_hbm,
    tri_in_hbm,
    gate_w_hbm,
    tri_out_hbm,
    out_ref,
    msa_ref,
    pair_ref,
    first_ref,
    second_ref,
    outer_ref,
    tri_in_ref,
    gate_w_ref,
    tri_out_ref,
    nm_ref,
    lt_ref,
    rt_ref,
    rg,
    wp_ref,
    x_ref,
    pm_ref,
    gate_ref,
    redge_ref,
    lall,
    rbuf,
    mst,
    accb,
    a_up,
    a_down,
    a_y,
    a_core,
    a_recv,
    in_sem,
    l_send,
    l_recv,
    up_sem,
    down_sem,
    line_recv,
    m_send,
    m_recv,
):
    S, I, J, R, C, half, channels = dims
    nr = R // C
    Z = R // 4
    zs = nr // 4
    rows = nr * 64
    parts = max(2, zs)

    r = lax.axis_index("row")
    c = lax.axis_index("col")
    core = lax.rem(r, 2)
    y = lax.rem(lax.div(r, 2), 2)
    z = lax.div(r, 4)
    def row_at(zz, yy, cc):
        return zz * 4 + yy * 2 + cc

    up_row = row_at(lax.rem(z + 1, Z), y, core)
    down_row = row_at(lax.rem(z + Z - 1, Z), y, core)
    y_row = row_at(z, 1 - y, core)
    core_row = row_at(z, y, 1 - core)

    loads = [
        pltpu.make_async_copy(src, dst, in_sem.at[n])
        for n, (src, dst) in enumerate(
            (
                (msa_hbm, msa_ref),
                (first_hbm, first_ref),
                (second_hbm, second_ref),
                (outer_hbm, outer_ref),
                (pair_hbm, pair_ref),
                (tri_in_hbm, tri_in_ref),
                (gate_w_hbm, gate_w_ref),
                (tri_out_hbm, tri_out_ref),
            )
        )
    ]
    for load in loads:
        load.start()

    barrier = pltpu.get_barrier_semaphore()
    greet = [(up_row, c), (down_row, c)]
    for k in range(C):
        for n in range(4):
            if k or n:
                greet.append((row_at(z, lax.rem(y + n // 2, 2), lax.rem(core + n, 2)), lax.rem(c + k, C)))
    for target in greet:
        pl.semaphore_signal(barrier, inc=1, device_id=target, device_id_type=MESH)

    for load in loads[:3]:
        load.wait()
    both = jnp.concatenate([first_ref[...], second_ref[...]], 0)
    both_h, both_l = split(both)
    both_hl = jnp.concatenate([both_h, both_l], 0)
    depth = msa_ref.shape[1]
    normed = layer_norm(msa_ref[...])
    for n in range(depth // 128):
        nm_ref[n] = normed[:, n * 128 : (n + 1) * 128]
    for m in range(I):
        xh, xl = split(
            jnp.concatenate([nm_ref[n, pl.ds(m, S, stride=I), :] for n in range(depth // 128)], 1)
        )
        t = dot_nt(both_hl, xh)
        t = t[: 2 * half] + t[2 * half :] + dot_nt(both_h, xl)
        lt_ref[m * half : (m + 1) * half, :] = t[:half] * (1.0 / S)
        rt_ref[m * half : (m + 1) * half, :] = t[half:]

    @pl.when(lax.div(r, nr) == c)
    def _():
        slot = lax.rem(r, nr)
        for b in range(half):
            rg[slot, b * I : (b + 1) * I, :] = rt_ref[pl.ds(b, I, stride=half), :]

    pl.semaphore_wait(barrier, len(greet))

    piece_rows = half * I // pieces

    def a_copy(slot, u, send, target):
        at = rg.at[slot, pl.ds(u * piece_rows, piece_rows)]
        return pltpu.make_async_remote_copy(
            src_ref=at,
            dst_ref=at,
            send_sem=send,
            recv_sem=a_recv.at[slot, u],
            device_id=(target, c),
            device_id_type=MESH,
        )

    def turned(t, zz):
        flip = (zz > c * zs).astype(jnp.int32)
        return t + flip * (zs - 1 - 2 * t)

    def a_links(t):
        zi = turned(t, z)
        source = c * zs + zi
        slot = zi * 4 + y * 2 + core
        return (
            slot,
            source,
            jnp.logical_and(z >= source, z < Z - 1),
            jnp.logical_and(z <= source, z > 0),
        )

    def a_line(t):
        slot, source, goes_up, goes_down = a_links(t)
        for u in range(pieces):

            @pl.when(z != source)
            def _():
                a_copy(slot, u, a_y.at[t, u], y_row).wait_recv()

            @pl.when(goes_up)
            def _():
                a_copy(slot, u, a_up.at[t, u], up_row).start()

            @pl.when(goes_down)
            def _():
                a_copy(slot, u, a_down.at[t, u], down_row).start()

            a_copy(slot, u, a_y.at[t, u], y_row).start()
            a_copy(slot, u, a_core.at[t, 0, u], core_row).start()

    def a_across(t):
        slot = turned(t, z) * 4 + (1 - y) * 2 + core
        for u in range(pieces):
            a_copy(slot, u, a_core.at[t, 1, u], core_row).wait_recv()
            a_copy(slot, u, a_core.at[t, 1, u], core_row).start()

    a_line(0)

    loads[3].wait()
    for b in range(half):
        wp_ref[b * half : (b + 1) * half, :] = outer_ref[pl.ds(b, half, stride=half), :]

    lt = lt_ref[...]
    lt_h, lt_l = split(lt)
    lt_hh = jnp.concatenate([lt_h, lt_h], 1)
    lane = lax.broadcasted_iota(jnp.int32, (half // 4, I, 128), 2)
    low64 = lane < 64
    low32 = lax.rem(lane, 64) < 32

    def outer_block(slot):
        rh, rl = split(rg[slot])
        o = dot_nt(jnp.concatenate([rh, rl], 1), lt_hh) + dot_nt(rh, lt_l)
        o = o.reshape(half // 4, 4, I, half * I)
        for h in range(half * I // 128):
            x = [o[:, q, :, h * 128 : (h + 1) * 128] for q in range(4)]
            w = [None] * 4
            for q in range(2):
                w[q] = jnp.where(low64, x[q], pltpu.roll(x[q + 2], 64, 2))
                w[q + 2] = jnp.where(low64, pltpu.roll(x[q], 64, 2), x[q + 2])
            v = [None] * 4
            for q in (0, 2):
                v[q] = jnp.where(low32, w[q], pltpu.roll(w[q + 1], 32, 2))
                v[q + 1] = jnp.where(low32, pltpu.roll(w[q], 96, 2), w[q + 1])
            for q in range(4):
                i = h * 4 + q
                for g in range(half // 4):
                    x_ref[slot, i * I : (i + 1) * I, g * 128 : (g + 1) * 128] = v[q][g]

    wh, wl = split(wp_ref[...])
    w_hl = jnp.concatenate([wh, wl], 1)
    for load in loads[4:]:
        load.wait()
    in_w = jnp.concatenate([tri_in_ref[...], gate_w_ref[...]], 1)
    in_h, in_l = split(in_w)
    in_hh = jnp.concatenate([in_h, in_h], 0)
    out_h, out_l = split(tri_out_ref[...])
    out_hh = jnp.concatenate([out_h, out_h], 0)
    ch = tri_out_ref.shape[0]
    group = 4 * 64

    def pair_group(zi):
        xh, xl = split(x_ref[pl.ds(zi * 4, 4)].reshape(group, half * half))
        t = dot_nn(xh, w_hl)
        t = t[:, :channels] + t[:, channels:] + dot_nn(xl, wh)
        own = jnp.concatenate(
            [
                pair_ref[pl.ds(pl.multiple_of(i * J + (zi * 4 + s) * I, I), I), :]
                for s in range(4)
                for i in range(I)
            ],
            0,
        )
        mid = own + t
        sl = pl.ds(pl.multiple_of(zi * group, group), group)
        pm_ref[sl, :] = mid
        nh, nl = split(layer_norm(mid))
        pr = dot_nn(jnp.concatenate([nh, nl], 1), in_hh) + dot_nn(nh, in_l)
        redge_ref[sl, :] = sigmoid(pr[:, 3 * ch : 4 * ch]) * pr[:, 2 * ch : 3 * ch]
        for s in range(4):
            for k in range(I):
                at = pl.multiple_of(zi * group + (s * I + k) * I, I)
                rbuf[z, pl.ds(at, I), :] = redge_ref[
                    pl.ds(zi * group + s * 64 + k, I, stride=I), :
                ]
        for n in range(parts // zs):
            send_on(0, zi * (parts // zs) + n)
        lall[2 * y + core, sl, :] = sigmoid(pr[:, ch : 2 * ch]) * pr[:, :ch]
        l_copy(0, zi).start()
        l_copy(1, zi).start()
        gate_ref[sl, :] = sigmoid(pr[:, 4 * ch :])

    part = rows // parts

    def line_copy(source, h, send, target):
        at = rbuf.at[source, pl.ds(pl.multiple_of(h * part, part), part)]
        return pltpu.make_async_remote_copy(
            src_ref=at,
            dst_ref=at,
            send_sem=send,
            recv_sem=line_recv.at[source, h],
            device_id=(target, c),
            device_id_type=MESH,
        )

    def line_up(t, h):
        return line_copy(z - t, h, up_sem.at[t, h], up_row)

    def line_down(t, h):
        return line_copy(z + t, h, down_sem.at[t, h], down_row)

    def send_on(t, h):
        @pl.when(jnp.logical_and(z >= t, z < Z - 1))
        def _():
            line_up(t, h).start()

        @pl.when(jnp.logical_and(z + t < Z, z > 0))
        def _():
            line_down(t, h).start()

    own_l = 2 * y + core

    def l_copy(n, zi):
        slot = own_l if n < 2 else 2 * (1 - y) + core
        at = lall.at[slot, pl.ds(pl.multiple_of(zi * group, group), group)]
        return pltpu.make_async_remote_copy(
            src_ref=at,
            dst_ref=at,
            send_sem=l_send.at[n, zi],
            recv_sem=l_recv.at[slot, zi],
            device_id=(y_row if n == 1 else core_row, c),
            device_id_type=MESH,
        )

    def l_arrived(slot, zi):
        at = lall.at[slot, pl.ds(pl.multiple_of(zi * group, group), group)]
        pltpu.make_async_remote_copy(
            src_ref=at,
            dst_ref=at,
            send_sem=l_send.at[0, zi],
            recv_sem=l_recv.at[slot, zi],
            device_id=(core_row, c),
            device_id_type=MESH,
        ).wait_recv()

    def part_order(source, n):
        if zs == 1:
            return n
        return turned(n, source)

    def piece(d, source, q):
        dest_col = lax.div(source, zs)
        slot = lax.rem(source, zs) * 4 + own_l
        target = row_at(z, lax.rem(y + q // 2, 2), lax.rem(core + q, 2))
        return (
            dest_col,
            slot,
            pltpu.make_async_remote_copy(
                src_ref=mst.at[d, q],
                dst_ref=accb.at[c, slot],
                send_sem=m_send.at[d, q],
                recv_sem=m_recv.at[c, slot],
                device_id=(target, dest_col),
                device_id_type=MESH,
            ),
        )

    def triangle(d, source, h, first, last):
        for pair in ((2, 3), (1, 0)):
            who = [2 * lax.rem(y + q // 2, 2) + lax.rem(core + q, 2) for q in pair]

            def step(s, acc):
                acc = list(acc)
                s = h * (nr // parts) + s
                for k in range(I):
                    rv = rbuf[source, pl.ds(pl.multiple_of((s * I + k) * I, I), I), :]
                    for n in range(2):
                        for i in range(I):
                            lv = lall[who[n], pl.ds(s * 64 + i * I + k, 1), :]
                            acc[n * I + i] = acc[n * I + i] + lv * rv
                return tuple(acc)

            if first:
                acc = tuple(jnp.zeros((I, channels), f32) for _ in range(2 * I))
            else:
                acc = tuple(
                    mst[d, q, i * I : (i + 1) * I, :] for q in pair for i in range(I)
                )
            acc = lax.fori_loop(0, nr // parts, step, acc)
            for n, q in enumerate(pair):
                for i in range(I):
                    mst[d, q, i * I : (i + 1) * I, :] = acc[n * I + i]
                if not last:
                    continue
                dest_col, slot, copy = piece(d, source, q)
                if q:
                    copy.start()
                else:

                    @pl.when(dest_col == c)
                    def _():
                        accb[c, slot] = mst[d, q]

                    @pl.when(dest_col != c)
                    def _():
                        copy.start()

    def finish(source, exists):
        @pl.when(jnp.logical_and(exists, lax.div(source, zs) == c))
        def _():
            base = lax.rem(source, zs) * 4

            def arrived(k, s):
                pltpu.make_async_remote_copy(
                    src_ref=mst.at[0, 0],
                    dst_ref=accb.at[k, s],
                    send_sem=m_send.at[0, 0],
                    recv_sem=m_recv.at[k, s],
                    device_id=(core_row, c),
                    device_id_type=MESH,
                ).wait_recv()

            for n in range(1, 4):
                arrived(c, base + 2 * lax.rem(y + n // 2, 2) + lax.rem(core + n, 2))
            for n in range(1, C):
                for s in range(4):
                    arrived(lax.rem(c + n, C), base + s)
            for s in range(0, 4, 2):
                mixed = accb[0, pl.ds(base + s, 2)].reshape(128, channels)
                for k in range(1, C):
                    mixed = mixed + accb[k, pl.ds(base + s, 2)].reshape(128, channels)
                nh, nl = split(layer_norm(mixed))
                t = dot_nn(jnp.concatenate([nh, nl], 1), out_hh) + dot_nn(nh, out_l)
                sl = pl.ds(pl.multiple_of((base + s) * 64, 64), 128)
                t = pm_ref[sl, :] + gate_ref[sl, :] * t
                for n in range(2):
                    for i in range(I):
                        at = pl.multiple_of(i * J + (base + s + n) * I, I)
                        out_ref[pl.ds(at, I), :] = t[(n * I + i) * I : (n * I + i + 1) * I]

    outer_block(a_links(0)[0])
    for t in range(1, zs):
        a_line(t)
    a_across(0)
    for t in range(zs):
        zi = turned(t, z)
        if t > 0:
            outer_block(zi * 4 + y * 2 + core)
        outer_block(zi * 4 + (1 - y) * 2 + core)
        for yy in (y, 1 - y):
            slot = zi * 4 + yy * 2 + 1 - core
            for u in range(pieces):
                a_copy(slot, u, a_core.at[t, 1, u], core_row).wait_recv()
            outer_block(slot)
        if t + 1 < zs:
            a_across(t + 1)
        pair_group(zi)

    for t in range(zs):
        zi = turned(t, z)
        l_arrived(2 * (1 - y) + core, zi)
        l_copy(2, zi).start()
    for t in range(zs):
        zi = turned(t, z)
        l_arrived(2 * y + 1 - core, zi)
        l_arrived(2 * (1 - y) + 1 - core, zi)
    for n in range(parts):
        triangle(0, z, part_order(z, n), n == 0, n == parts - 1)
    for t in range(1, Z):
        for n in range(parts):
            below = part_order(z - t, n)
            above = part_order(z + t, n)

            @pl.when(z >= t)
            def _():
                line_up(t, below).wait_recv()

                @pl.when(z < Z - 1)
                def _():
                    line_up(t, below).start()

            @pl.when(z + t < Z)
            def _():
                line_down(t, above).wait_recv()

                @pl.when(z > 0)
                def _():
                    line_down(t, above).start()

            @pl.when(z >= t)
            def _():
                triangle(t, z - t, below, n == 0, n == parts - 1)

            @pl.when(z + t < Z)
            def _():
                triangle(Z - 1 + t, z + t, above, n == 0, n == parts - 1)

        if t == 1:
            finish(z, z >= 0)
        else:
            finish(z - t + 1, z >= t - 1)
            finish(z + t - 1, z + t - 1 < Z)
    finish(z - Z + 1, z >= Z - 1)
    finish(z + Z - 1, z < 1)

    for t in range(zs):
        slot, source, goes_up, goes_down = a_links(t)
        across = turned(t, z) * 4 + (1 - y) * 2 + core
        for u in range(pieces):

            @pl.when(goes_up)
            def _():
                a_copy(slot, u, a_up.at[t, u], up_row).wait_send()

            @pl.when(goes_down)
            def _():
                a_copy(slot, u, a_down.at[t, u], down_row).wait_send()

            a_copy(slot, u, a_y.at[t, u], y_row).wait_send()
            a_copy(slot, u, a_core.at[t, 0, u], core_row).wait_send()
            a_copy(across, u, a_core.at[t, 1, u], core_row).wait_send()
        for n in range(3):
            l_copy(n, t).wait_send()
    for t in range(Z):
        for h in range(parts):

            @pl.when(jnp.logical_and(z >= t, z < Z - 1))
            def _():
                line_up(t, h).wait_send()

            @pl.when(jnp.logical_and(z + t < Z, z > 0))
            def _():
                line_down(t, h).wait_send()

    def pieces_left(d, source):
        for q in range(4):
            dest_col, _, copy = piece(d, source, q)
            if q:
                copy.wait_send()
            else:

                @pl.when(dest_col != c)
                def _():
                    copy.wait_send()

    pieces_left(0, z)
    for t in range(1, Z):

        @pl.when(z >= t)
        def _():
            pieces_left(t, z - t)

        @pl.when(z + t < Z)
        def _():
            pieces_left(Z - 1 + t, z + t)


def per_device(R, C, msa, pair, first, second, outer_w, tri_in, gate_w, tri_out):
    S, I, depth = msa.shape
    J, channels = pair.shape[1:]
    half = first.shape[1]
    nr = R // C
    zs = nr // 4
    Z = R // 4
    rows = nr * I * I
    parts = max(2, zs)
    operands = (
        msa.reshape(S * I, depth),
        pair.reshape(I * J, channels),
        first.T,
        second.T,
        outer_w,
        tri_in,
        gate_w,
        tri_out,
    )
    dma = pltpu.SemaphoreType.DMA
    out = pl.pallas_call(
        functools.partial(kernel, (S, I, J, R, C, half, channels)),
        out_shape=jax.ShapeDtypeStruct((I * J, channels), f32),
        in_specs=[pl.BlockSpec(memory_space=pltpu.HBM)] * 8,
        out_specs=pl.BlockSpec(memory_space=pltpu.VMEM),
        scratch_shapes=[pltpu.VMEM(x.shape, f32) for x in operands]
        + [
            pltpu.VMEM((depth // 128, S * I, 128), f32),
            pltpu.VMEM((I * half, S), f32),
            pltpu.VMEM((I * half, S), f32),
            pltpu.VMEM((nr, half * I, S), f32),
            pltpu.VMEM((half * half, channels), f32),
            pltpu.VMEM((nr, I * I, half * half), f32),
            pltpu.VMEM((rows, channels), f32),
            pltpu.VMEM((rows, channels), f32),
            pltpu.VMEM((rows, channels), f32),
            pltpu.VMEM((4, rows, channels), f32),
            pltpu.VMEM((Z, rows, channels), f32),
            pltpu.VMEM((2 * Z - 1, 4, I * I, channels), f32),
            pltpu.VMEM((C, nr, I * I, channels), f32),
            dma((zs, pieces)),
            dma((zs, pieces)),
            dma((zs, pieces)),
            dma((zs, 2, pieces)),
            dma((nr, pieces)),
            dma((len(operands),)),
            dma((3, zs)),
            dma((4, zs)),
            dma((Z, parts)),
            dma((Z, parts)),
            dma((Z, parts)),
            dma((2 * Z - 1, 4)),
            dma((C, nr)),
        ],
        compiler_params=pltpu.CompilerParams(
            collective_id=0, has_side_effects=True, vmem_limit_bytes=62 * 1024 * 1024
        ),
        cost_estimate=pl.CostEstimate(
            flops=6 * 180 * 10**6, bytes_accessed=3 * 10**6, transcendentals=200000
        ),
    )(*operands)
    return out.reshape(I, J, channels)


def solution(mesh):
    placed = (P(None, "row", None), P("row", "col", None), P(), P(), P(), P(), P(), P())
    return jax.shard_map(
        functools.partial(per_device, mesh.shape["row"], mesh.shape["col"]),
        mesh=mesh,
        in_specs=placed,
        out_specs=P("row", "col", None),
        check_vma=False,
    )
```

```python
import functools

import jax
import jax.numpy as jnp
from jax import lax
from jax.experimental import pallas as pl
from jax.experimental.pallas import tpu as pltpu
from jax.sharding import PartitionSpec as P

epsilon = 1e-05
MESH = pl.DeviceIdType.MESH
f32 = jnp.float32
bf16 = jnp.bfloat16
pieces = 4


def split(x):
    hi = x.astype(bf16)
    lo = (x - hi.astype(f32)).astype(bf16)
    return hi, lo


def dot_nn(a, b):
    return lax.dot_general(a, b, (((1,), (0,)), ((), ())), preferred_element_type=f32)


def layer_norm(values):
    average = jnp.mean(values, -1, keepdims=True)
    centred = values - average
    variance = jnp.mean(centred * centred, -1, keepdims=True)
    return centred * lax.rsqrt(variance + epsilon)


def sigmoid(x):
    return 1.0 / (1.0 + jnp.exp(-x))


def kernel(
    dims,
    msa_hbm,
    pair_hbm,
    first_hbm,
    second_hbm,
    outer_hbm,
    tri_in_hbm,
    gate_w_hbm,
    tri_out_hbm,
    out_ref,
    msa_ref,
    pair_ref,
    first_ref,
    second_ref,
    outer_ref,
    tri_in_ref,
    gate_w_ref,
    tri_out_ref,
    nm_ref,
    left_ref,
    lt_ref,
    rt_ref,
    rg,
    wp_ref,
    x_ref,
    pm_ref,
    gate_ref,
    redge_ref,
    lall,
    rbuf,
    mst,
    accb,
    a_up,
    a_down,
    a_y,
    a_core,
    a_recv,
    in_sem,
    l_send,
    l_recv,
    up_sem,
    down_sem,
    line_recv,
    m_send,
    m_recv,
):
    S, I, J, R, C, half, channels = dims
    nr = R // C
    Z = R // 4
    zs = nr // 4
    rows = nr * 64
    parts = max(2, zs)

    r = lax.axis_index("row")
    c = lax.axis_index("col")
    core = lax.rem(r, 2)
    y = lax.rem(lax.div(r, 2), 2)
    z = lax.div(r, 4)
    def row_at(zz, yy, cc):
        return zz * 4 + yy * 2 + cc

    up_row = row_at(lax.rem(z + 1, Z), y, core)
    down_row = row_at(lax.rem(z + Z - 1, Z), y, core)
    y_row = row_at(z, 1 - y, core)
    core_row = row_at(z, y, 1 - core)

    loads = [
        pltpu.make_async_copy(src, dst, in_sem.at[n])
        for n, (src, dst) in enumerate(
            (
                (msa_hbm, msa_ref),
                (first_hbm, first_ref),
                (second_hbm, second_ref),
                (outer_hbm, outer_ref),
                (pair_hbm, pair_ref),
                (tri_in_hbm, tri_in_ref),
                (gate_w_hbm, gate_w_ref),
                (tri_out_hbm, tri_out_ref),
            )
        )
    ]
    for load in loads:
        load.start()

    barrier = pltpu.get_barrier_semaphore()
    greet = [(up_row, c), (down_row, c)]
    for k in range(C):
        for n in range(4):
            if k or n:
                greet.append((row_at(z, lax.rem(y + n // 2, 2), lax.rem(core + n, 2)), lax.rem(c + k, C)))
    for target in greet:
        pl.semaphore_signal(barrier, inc=1, device_id=target, device_id_type=MESH)

    for load in loads[:3]:
        load.wait()
    both_h, both_l = split(jnp.concatenate([first_ref[...], second_ref[...]], 0).T)
    both_hl = jnp.concatenate([both_h, both_l], 1)
    block = 256
    for n in range(S * I // block):
        sl = slice(n * block, (n + 1) * block)
        xh, xl = split(layer_norm(msa_ref[sl, :]))
        t = dot_nn(xh, both_hl)
        t = t + dot_nn(xl, jnp.concatenate([both_h, jnp.zeros_like(both_h)], 1))
        nm_ref[sl, :] = t + pltpu.roll(t, 2 * half, 1)
    for m in range(I):
        t = nm_ref[pl.ds(m, S, stride=I), :].T
        lt_ref[m * half : (m + 1) * half, :] = t[:half] * (1.0 / S)
        rt_ref[m * half : (m + 1) * half, :] = t[half : 2 * half]

    @pl.when(lax.div(r, nr) == c)
    def _():
        slot = lax.rem(r, nr)
        for b in range(half):
            rg[slot, b * I : (b + 1) * I, :] = rt_ref[pl.ds(b, I, stride=half), :]

    pl.semaphore_wait(barrier, len(greet))

    piece_rows = half * I // pieces

    def a_copy(slot, u, send, target):
        at = rg.at[slot, pl.ds(u * piece_rows, piece_rows)]
        return pltpu.make_async_remote_copy(
            src_ref=at,
            dst_ref=at,
            send_sem=send,
            recv_sem=a_recv.at[slot, u],
            device_id=(target, c),
            device_id_type=MESH,
        )

    def turned(t, zz):
        flip = (zz > c * zs).astype(jnp.int32)
        return t + flip * (zs - 1 - 2 * t)

    def a_links(t):
        zi = turned(t, z)
        source = c * zs + zi
        slot = zi * 4 + y * 2 + core
        return (
            slot,
            source,
            jnp.logical_and(z >= source, z < Z - 1),
            jnp.logical_and(z <= source, z > 0),
        )

    def a_line(t):
        slot, source, goes_up, goes_down = a_links(t)
        for u in range(pieces):

            @pl.when(z != source)
            def _():
                a_copy(slot, u, a_y.at[t, u], y_row).wait_recv()

            @pl.when(goes_up)
            def _():
                a_copy(slot, u, a_up.at[t, u], up_row).start()

            @pl.when(goes_down)
            def _():
                a_copy(slot, u, a_down.at[t, u], down_row).start()

            a_copy(slot, u, a_y.at[t, u], y_row).start()
            a_copy(slot, u, a_core.at[t, 0, u], core_row).start()

    def a_across(t):
        slot = turned(t, z) * 4 + (1 - y) * 2 + core
        for u in range(pieces):
            a_copy(slot, u, a_core.at[t, 1, u], core_row).wait_recv()
            a_copy(slot, u, a_core.at[t, 1, u], core_row).start()

    a_line(0)

    loads[3].wait()
    for b in range(half):
        wp_ref[b * half : (b + 1) * half, :] = outer_ref[pl.ds(b, half, stride=half), :]

    lt_h, lt_l = split(lt_ref[...].T)
    left_ref[:S, :] = lt_h
    left_ref[S : 2 * S, :] = lt_h
    left_ref[2 * S :, :] = lt_l
    lane = lax.broadcasted_iota(jnp.int32, (half // 4, I, 128), 2)
    low64 = lane < 64
    low32 = lax.rem(lane, 64) < 32

    def outer_block(slot):
        rh, rl = split(rg[slot])
        o = dot_nn(jnp.concatenate([rh, rl], 1), left_ref[: 2 * S, :])
        o = o + dot_nn(rh, left_ref[2 * S :, :])
        o = o.reshape(half // 4, 4, I, half * I)
        for h in range(half * I // 128):
            x = [o[:, q, :, h * 128 : (h + 1) * 128] for q in range(4)]
            w = [None] * 4
            for q in range(2):
                w[q] = jnp.where(low64, x[q], pltpu.roll(x[q + 2], 64, 2))
                w[q + 2] = jnp.where(low64, pltpu.roll(x[q], 64, 2), x[q + 2])
            v = [None] * 4
            for q in (0, 2):
                v[q] = jnp.where(low32, w[q], pltpu.roll(w[q + 1], 32, 2))
                v[q + 1] = jnp.where(low32, pltpu.roll(w[q], 96, 2), w[q + 1])
            for q in range(4):
                i = h * 4 + q
                for g in range(half // 4):
                    x_ref[slot, i * I : (i + 1) * I, g * 128 : (g + 1) * 128] = v[q][g]

    wh, wl = split(wp_ref[...])
    w_hl = jnp.concatenate([wh, wl], 1)
    for load in loads[4:]:
        load.wait()
    ch = tri_out_ref.shape[0]
    right_h, right_l = split(tri_in_ref[:, 2 * ch :])
    right_hh = jnp.concatenate([right_h, right_h], 0)
    in_h, in_l = split(jnp.concatenate([tri_in_ref[:, : 2 * ch], gate_w_ref[...]], 1))
    in_hh = jnp.concatenate([in_h, in_h], 0)
    out_h, out_l = split(tri_out_ref[...])
    out_hh = jnp.concatenate([out_h, out_h], 0)
    group = 4 * 64

    def pair_group(zi):
        xh, xl = split(x_ref[pl.ds(zi * 4, 4)].reshape(group, half * half))
        t = dot_nn(xh, w_hl)
        t = t[:, :channels] + t[:, channels:] + dot_nn(xl, wh)
        own = jnp.concatenate(
            [
                pair_ref[pl.ds(pl.multiple_of(i * J + (zi * 4 + s) * I, I), I), :]
                for s in range(4)
                for i in range(I)
            ],
            0,
        )
        mid = own + t
        sl = pl.ds(pl.multiple_of(zi * group, group), group)
        pm_ref[sl, :] = mid
        nh, nl = split(layer_norm(mid))
        nhl = jnp.concatenate([nh, nl], 1)
        pr = dot_nn(nhl, right_hh) + dot_nn(nh, right_l)
        redge_ref[sl, :] = sigmoid(pr[:, ch:]) * pr[:, :ch]
        for s in range(4):
            for k in range(I):
                at = pl.multiple_of(zi * group + (s * I + k) * I, I)
                rbuf[z, pl.ds(at, I), :] = redge_ref[
                    pl.ds(zi * group + s * 64 + k, I, stride=I), :
                ]
        for n in range(parts // zs):
            send_on(0, zi * (parts // zs) + n)
        pr = dot_nn(nhl, in_hh) + dot_nn(nh, in_l)
        lall[2 * y + core, sl, :] = sigmoid(pr[:, ch : 2 * ch]) * pr[:, :ch]
        l_copy(0, zi).start()
        l_copy(1, zi).start()
        gate_ref[sl, :] = sigmoid(pr[:, 2 * ch :])

    part = rows // parts

    def line_copy(source, h, send, target):
        at = rbuf.at[source, pl.ds(pl.multiple_of(h * part, part), part)]
        return pltpu.make_async_remote_copy(
            src_ref=at,
            dst_ref=at,
            send_sem=send,
            recv_sem=line_recv.at[source, h],
            device_id=(target, c),
            device_id_type=MESH,
        )

    def line_up(t, h):
        return line_copy(z - t, h, up_sem.at[t, h], up_row)

    def line_down(t, h):
        return line_copy(z + t, h, down_sem.at[t, h], down_row)

    def send_on(t, h):
        @pl.when(jnp.logical_and(z >= t, z < Z - 1))
        def _():
            line_up(t, h).start()

        @pl.when(jnp.logical_and(z + t < Z, z > 0))
        def _():
            line_down(t, h).start()

    own_l = 2 * y + core

    def l_copy(n, zi):
        slot = own_l if n < 2 else 2 * (1 - y) + core
        at = lall.at[slot, pl.ds(pl.multiple_of(zi * group, group), group)]
        return pltpu.make_async_remote_copy(
            src_ref=at,
            dst_ref=at,
            send_sem=l_send.at[n, zi],
            recv_sem=l_recv.at[slot, zi],
            device_id=(y_row if n == 1 else core_row, c),
            device_id_type=MESH,
        )

    def l_arrived(slot, zi):
        at = lall.at[slot, pl.ds(pl.multiple_of(zi * group, group), group)]
        pltpu.make_async_remote_copy(
            src_ref=at,
            dst_ref=at,
            send_sem=l_send.at[0, zi],
            recv_sem=l_recv.at[slot, zi],
            device_id=(core_row, c),
            device_id_type=MESH,
        ).wait_recv()

    def part_order(source, n):
        if zs == 1:
            return n
        return turned(n, source)

    def piece(d, source, q):
        dest_col = lax.div(source, zs)
        slot = lax.rem(source, zs) * 4 + own_l
        target = row_at(z, lax.rem(y + q // 2, 2), lax.rem(core + q, 2))
        return (
            dest_col,
            slot,
            pltpu.make_async_remote_copy(
                src_ref=mst.at[d, q],
                dst_ref=accb.at[c, slot],
                send_sem=m_send.at[d, q],
                recv_sem=m_recv.at[c, slot],
                device_id=(target, dest_col),
                device_id_type=MESH,
            ),
        )

    def triangle(d, source, h, first, last):
        for pair in ((2, 3), (1, 0)):
            who = [2 * lax.rem(y + q // 2, 2) + lax.rem(core + q, 2) for q in pair]

            def step(s, acc):
                acc = list(acc)
                s = h * (nr // parts) + s
                for k in range(I):
                    rv = rbuf[source, pl.ds(pl.multiple_of((s * I + k) * I, I), I), :]
                    for n in range(2):
                        for i in range(I):
                            lv = lall[who[n], pl.ds(s * 64 + i * I + k, 1), :]
                            acc[n * I + i] = acc[n * I + i] + lv * rv
                return tuple(acc)

            if first:
                acc = tuple(jnp.zeros((I, channels), f32) for _ in range(2 * I))
            else:
                acc = tuple(
                    mst[d, q, i * I : (i + 1) * I, :] for q in pair for i in range(I)
                )
            acc = lax.fori_loop(0, nr // parts, step, acc)
            for n, q in enumerate(pair):
                for i in range(I):
                    mst[d, q, i * I : (i + 1) * I, :] = acc[n * I + i]
                if not last:
                    continue
                dest_col, slot, copy = piece(d, source, q)
                if q:
                    copy.start()
                else:

                    @pl.when(dest_col == c)
                    def _():
                        accb[c, slot] = mst[d, q]

                    @pl.when(dest_col != c)
                    def _():
                        copy.start()

    def finish(source, exists):
        @pl.when(jnp.logical_and(exists, lax.div(source, zs) == c))
        def _():
            base = lax.rem(source, zs) * 4

            def arrived(k, s):
                pltpu.make_async_remote_copy(
                    src_ref=mst.at[0, 0],
                    dst_ref=accb.at[k, s],
                    send_sem=m_send.at[0, 0],
                    recv_sem=m_recv.at[k, s],
                    device_id=(core_row, c),
                    device_id_type=MESH,
                ).wait_recv()

            for n in range(1, 4):
                arrived(c, base + 2 * lax.rem(y + n // 2, 2) + lax.rem(core + n, 2))
            for n in range(1, C):
                for s in range(4):
                    arrived(lax.rem(c + n, C), base + s)
            for s in range(0, 4, 2):
                mixed = accb[0, pl.ds(base + s, 2)].reshape(128, channels)
                for k in range(1, C):
                    mixed = mixed + accb[k, pl.ds(base + s, 2)].reshape(128, channels)
                nh, nl = split(layer_norm(mixed))
                t = dot_nn(jnp.concatenate([nh, nl], 1), out_hh) + dot_nn(nh, out_l)
                sl = pl.ds(pl.multiple_of((base + s) * 64, 64), 128)
                t = pm_ref[sl, :] + gate_ref[sl, :] * t
                for n in range(2):
                    for i in range(I):
                        at = pl.multiple_of(i * J + (base + s + n) * I, I)
                        out_ref[pl.ds(at, I), :] = t[(n * I + i) * I : (n * I + i + 1) * I]

    outer_block(a_links(0)[0])
    for t in range(1, zs):
        a_line(t)
    a_across(0)
    for t in range(zs):
        zi = turned(t, z)
        if t > 0:
            outer_block(zi * 4 + y * 2 + core)
        outer_block(zi * 4 + (1 - y) * 2 + core)
        for yy in (y, 1 - y):
            slot = zi * 4 + yy * 2 + 1 - core
            for u in range(pieces):
                a_copy(slot, u, a_core.at[t, 1, u], core_row).wait_recv()
            outer_block(slot)
        if t + 1 < zs:
            a_across(t + 1)
        pair_group(zi)

    for t in range(zs):
        zi = turned(t, z)
        l_arrived(2 * (1 - y) + core, zi)
        l_copy(2, zi).start()
    for t in range(zs):
        zi = turned(t, z)
        l_arrived(2 * y + 1 - core, zi)
        l_arrived(2 * (1 - y) + 1 - core, zi)
    for n in range(parts):
        triangle(0, z, part_order(z, n), n == 0, n == parts - 1)
    for t in range(1, Z):
        for n in range(parts):
            below = part_order(z - t, n)
            above = part_order(z + t, n)

            @pl.when(z >= t)
            def _():
                line_up(t, below).wait_recv()

                @pl.when(z < Z - 1)
                def _():
                    line_up(t, below).start()

            @pl.when(z + t < Z)
            def _():
                line_down(t, above).wait_recv()

                @pl.when(z > 0)
                def _():
                    line_down(t, above).start()

            @pl.when(z >= t)
            def _():
                triangle(t, z - t, below, n == 0, n == parts - 1)

            @pl.when(z + t < Z)
            def _():
                triangle(Z - 1 + t, z + t, above, n == 0, n == parts - 1)

        if t == 1:
            finish(z, z >= 0)
        else:
            finish(z - t + 1, z >= t - 1)
            finish(z + t - 1, z + t - 1 < Z)
    finish(z - Z + 1, z >= Z - 1)
    finish(z + Z - 1, z < 1)

    for t in range(zs):
        slot, source, goes_up, goes_down = a_links(t)
        across = turned(t, z) * 4 + (1 - y) * 2 + core
        for u in range(pieces):

            @pl.when(goes_up)
            def _():
                a_copy(slot, u, a_up.at[t, u], up_row).wait_send()

            @pl.when(goes_down)
            def _():
                a_copy(slot, u, a_down.at[t, u], down_row).wait_send()

            a_copy(slot, u, a_y.at[t, u], y_row).wait_send()
            a_copy(slot, u, a_core.at[t, 0, u], core_row).wait_send()
            a_copy(across, u, a_core.at[t, 1, u], core_row).wait_send()
        for n in range(3):
            l_copy(n, t).wait_send()
    for t in range(Z):
        for h in range(parts):

            @pl.when(jnp.logical_and(z >= t, z < Z - 1))
            def _():
                line_up(t, h).wait_send()

            @pl.when(jnp.logical_and(z + t < Z, z > 0))
            def _():
                line_down(t, h).wait_send()

    def pieces_left(d, source):
        for q in range(4):
            dest_col, _, copy = piece(d, source, q)
            if q:
                copy.wait_send()
            else:

                @pl.when(dest_col != c)
                def _():
                    copy.wait_send()

    pieces_left(0, z)
    for t in range(1, Z):

        @pl.when(z >= t)
        def _():
            pieces_left(t, z - t)

        @pl.when(z + t < Z)
        def _():
            pieces_left(Z - 1 + t, z + t)


def per_device(R, C, msa, pair, first, second, outer_w, tri_in, gate_w, tri_out):
    S, I, depth = msa.shape
    J, channels = pair.shape[1:]
    half = first.shape[1]
    nr = R // C
    zs = nr // 4
    Z = R // 4
    rows = nr * I * I
    parts = max(2, zs)
    operands = (
        msa.reshape(S * I, depth),
        pair.reshape(I * J, channels),
        first.T,
        second.T,
        outer_w,
        tri_in,
        gate_w,
        tri_out,
    )
    dma = pltpu.SemaphoreType.DMA
    out = pl.pallas_call(
        functools.partial(kernel, (S, I, J, R, C, half, channels)),
        out_shape=jax.ShapeDtypeStruct((I * J, channels), f32),
        in_specs=[pl.BlockSpec(memory_space=pltpu.HBM)] * 8,
        out_specs=pl.BlockSpec(memory_space=pltpu.VMEM),
        scratch_shapes=[pltpu.VMEM(x.shape, f32) for x in operands]
        + [
            pltpu.VMEM((S * I, 4 * half), f32),
            pltpu.VMEM((3 * S, I * half), bf16),
            pltpu.VMEM((I * half, S), f32),
            pltpu.VMEM((I * half, S), f32),
            pltpu.VMEM((nr, half * I, S), f32),
            pltpu.VMEM((half * half, channels), f32),
            pltpu.VMEM((nr, I * I, half * half), f32),
            pltpu.VMEM((rows, channels), f32),
            pltpu.VMEM((rows, channels), f32),
            pltpu.VMEM((rows, channels), f32),
            pltpu.VMEM((4, rows, channels), f32),
            pltpu.VMEM((Z, rows, channels), f32),
            pltpu.VMEM((2 * Z - 1, 4, I * I, channels), f32),
            pltpu.VMEM((C, nr, I * I, channels), f32),
            dma((zs, pieces)),
            dma((zs, pieces)),
            dma((zs, pieces)),
            dma((zs, 2, pieces)),
            dma((nr, pieces)),
            dma((len(operands),)),
            dma((3, zs)),
            dma((4, zs)),
            dma((Z, parts)),
            dma((Z, parts)),
            dma((Z, parts)),
            dma((2 * Z - 1, 4)),
            dma((C, nr)),
        ],
        compiler_params=pltpu.CompilerParams(
            collective_id=0, has_side_effects=True, vmem_limit_bytes=62 * 1024 * 1024
        ),
        cost_estimate=pl.CostEstimate(
            flops=6 * 180 * 10**6, bytes_accessed=3 * 10**6, transcendentals=200000
        ),
    )(*operands)
    return out.reshape(I, J, channels)


def solution(mesh):
    placed = (P(None, "row", None), P("row", "col", None), P(), P(), P(), P(), P(), P())
    return jax.shard_map(
        functools.partial(per_device, mesh.shape["row"], mesh.shape["col"]),
        mesh=mesh,
        in_specs=placed,
        out_specs=P("row", "col", None),
        check_vma=False,
    )
```

```python
import functools

import jax
import jax.numpy as jnp
from jax import lax
from jax.experimental import pallas as pl
from jax.experimental.pallas import tpu as pltpu
from jax.sharding import PartitionSpec as P

epsilon = 1e-05
MESH = pl.DeviceIdType.MESH
f32 = jnp.float32
bf16 = jnp.bfloat16
pieces = 4


def split(x):
    hi = x.astype(bf16)
    lo = (x - hi.astype(f32)).astype(bf16)
    return hi, lo


def dot_nn(a, b):
    return lax.dot_general(a, b, (((1,), (0,)), ((), ())), preferred_element_type=f32)


def dot_nt(a, b):
    return lax.dot_general(a, b, (((1,), (1,)), ((), ())), preferred_element_type=f32)


def layer_norm(values):
    average = jnp.mean(values, -1, keepdims=True)
    centred = values - average
    variance = jnp.mean(centred * centred, -1, keepdims=True)
    return centred * lax.rsqrt(variance + epsilon)


def sigmoid(x):
    return 1.0 / (1.0 + jnp.exp(-x))


def kernel(
    dims,
    msa_hbm,
    pair_hbm,
    first_hbm,
    second_hbm,
    outer_hbm,
    tri_in_hbm,
    gate_w_hbm,
    tri_out_hbm,
    out_ref,
    msa_ref,
    pair_ref,
    first_ref,
    second_ref,
    outer_ref,
    tri_in_ref,
    gate_w_ref,
    tri_out_ref,
    nm_ref,
    lt_ref,
    rt_ref,
    rg,
    wp_ref,
    x_ref,
    pm_ref,
    gate_ref,
    redge_ref,
    lall,
    rbuf,
    mst,
    accb,
    a_up,
    a_down,
    a_y,
    a_core,
    a_recv,
    in_sem,
    l_send,
    l_recv,
    up_sem,
    down_sem,
    line_recv,
    m_send,
    m_recv,
):
    S, I, J, R, C, half, channels = dims
    nr = R // C
    Z = R // 4
    zs = nr // 4
    rows = nr * 64
    parts = max(2, zs)

    r = lax.axis_index("row")
    c = lax.axis_index("col")
    core = lax.rem(r, 2)
    y = lax.rem(lax.div(r, 2), 2)
    z = lax.div(r, 4)
    def row_at(zz, yy, cc):
        return zz * 4 + yy * 2 + cc

    up_row = row_at(lax.rem(z + 1, Z), y, core)
    down_row = row_at(lax.rem(z + Z - 1, Z), y, core)
    y_row = row_at(z, 1 - y, core)
    core_row = row_at(z, y, 1 - core)

    loads = [
        pltpu.make_async_copy(src, dst, in_sem.at[n])
        for n, (src, dst) in enumerate(
            (
                (msa_hbm, msa_ref),
                (first_hbm, first_ref),
                (second_hbm, second_ref),
                (outer_hbm, outer_ref),
                (pair_hbm, pair_ref),
                (tri_in_hbm, tri_in_ref),
                (gate_w_hbm, gate_w_ref),
                (tri_out_hbm, tri_out_ref),
            )
        )
    ]
    for load in loads:
        load.start()

    barrier = pltpu.get_barrier_semaphore()
    greet = [(up_row, c), (down_row, c)]
    for k in range(C):
        for n in range(4):
            if k or n:
                greet.append((row_at(z, lax.rem(y + n // 2, 2), lax.rem(core + n, 2)), lax.rem(c + k, C)))
    for target in greet:
        pl.semaphore_signal(barrier, inc=1, device_id=target, device_id_type=MESH)

    for load in loads[:3]:
        load.wait()
    both = jnp.concatenate([first_ref[...], second_ref[...]], 0)
    both_h, both_l = split(both)
    both_hl = jnp.concatenate([both_h, both_l], 0)
    depth = msa_ref.shape[1]
    normed = layer_norm(msa_ref[...])
    for n in range(depth // 128):
        nm_ref[n] = normed[:, n * 128 : (n + 1) * 128]
    for m in range(I):
        xh, xl = split(
            jnp.concatenate([nm_ref[n, pl.ds(m, S, stride=I), :] for n in range(depth // 128)], 1)
        )
        t = dot_nt(both_hl, xh)
        t = t[: 2 * half] + t[2 * half :] + dot_nt(both_h, xl)
        lt_ref[m * half : (m + 1) * half, :] = t[:half] * (1.0 / S)
        rt_ref[m * half : (m + 1) * half, :] = t[half:]

    @pl.when(lax.div(r, nr) == c)
    def _():
        slot = lax.rem(r, nr)
        for b in range(half):
            rg[slot, b * I : (b + 1) * I, :] = rt_ref[pl.ds(b, I, stride=half), :]

    pl.semaphore_wait(barrier, len(greet))

    piece_rows = half * I // pieces

    def a_copy(slot, u, send, target):
        at = rg.at[slot, pl.ds(u * piece_rows, piece_rows)]
        return pltpu.make_async_remote_copy(
            src_ref=at,
            dst_ref=at,
            send_sem=send,
            recv_sem=a_recv.at[slot, u],
            device_id=(target, c),
            device_id_type=MESH,
        )

    def turned(t, zz):
        flip = (zz > c * zs).astype(jnp.int32)
        return t + flip * (zs - 1 - 2 * t)

    def a_links(t):
        zi = turned(t, z)
        source = c * zs + zi
        slot = zi * 4 + y * 2 + core
        return (
            slot,
            source,
            jnp.logical_and(z >= source, z < Z - 1),
            jnp.logical_and(z <= source, z > 0),
        )

    def a_line(t):
        slot, source, goes_up, goes_down = a_links(t)
        for u in range(pieces):

            @pl.when(z != source)
            def _():
                a_copy(slot, u, a_y.at[t, u], y_row).wait_recv()

            @pl.when(goes_up)
            def _():
                a_copy(slot, u, a_up.at[t, u], up_row).start()

            @pl.when(goes_down)
            def _():
                a_copy(slot, u, a_down.at[t, u], down_row).start()

            a_copy(slot, u, a_y.at[t, u], y_row).start()
            a_copy(slot, u, a_core.at[t, 0, u], core_row).start()

    def a_across(t):
        slot = turned(t, z) * 4 + (1 - y) * 2 + core
        for u in range(pieces):
            a_copy(slot, u, a_core.at[t, 1, u], core_row).wait_recv()
            a_copy(slot, u, a_core.at[t, 1, u], core_row).start()

    a_line(0)

    loads[3].wait()
    for b in range(half):
        wp_ref[b * half : (b + 1) * half, :] = outer_ref[pl.ds(b, half, stride=half), :]

    lt = lt_ref[...]
    lt_h, lt_l = split(lt)
    lt_hh = jnp.concatenate([lt_h, lt_h], 1)
    lane = lax.broadcasted_iota(jnp.int32, (half // 4, I, 128), 2)
    low64 = lane < 64
    low32 = lax.rem(lane, 64) < 32

    def outer_block(slot):
        rh, rl = split(rg[slot])
        o = dot_nt(jnp.concatenate([rh, rl], 1), lt_hh) + dot_nt(rh, lt_l)
        o = o.reshape(half // 4, 4, I, half * I)
        for h in range(half * I // 128):
            x = [o[:, q, :, h * 128 : (h + 1) * 128] for q in range(4)]
            w = [None] * 4
            for q in range(2):
                w[q] = jnp.where(low64, x[q], pltpu.roll(x[q + 2], 64, 2))
                w[q + 2] = jnp.where(low64, pltpu.roll(x[q], 64, 2), x[q + 2])
            v = [None] * 4
            for q in (0, 2):
                v[q] = jnp.where(low32, w[q], pltpu.roll(w[q + 1], 32, 2))
                v[q + 1] = jnp.where(low32, pltpu.roll(w[q], 96, 2), w[q + 1])
            for q in range(4):
                i = h * 4 + q
                for g in range(half // 4):
                    x_ref[slot, i * I : (i + 1) * I, g * 128 : (g + 1) * 128] = v[q][g]

    wh, wl = split(wp_ref[...])
    w_hl = jnp.concatenate([wh, wl], 1)
    for load in loads[4:]:
        load.wait()
    in_w = jnp.concatenate([tri_in_ref[...], gate_w_ref[...]], 1)
    in_h, in_l = split(in_w)
    in_hh = jnp.concatenate([in_h, in_h], 0)
    out_h, out_l = split(tri_out_ref[...])
    out_hh = jnp.concatenate([out_h, out_h], 0)
    ch = tri_out_ref.shape[0]
    group = 4 * 64

    def pair_group(zi):
        xh, xl = split(x_ref[pl.ds(zi * 4, 4)].reshape(group, half * half))
        t = dot_nn(xh, w_hl)
        t = t[:, :channels] + t[:, channels:] + dot_nn(xl, wh)
        own = jnp.concatenate(
            [
                pair_ref[pl.ds(pl.multiple_of(i * J + (zi * 4 + s) * I, I), I), :]
                for s in range(4)
                for i in range(I)
            ],
            0,
        )
        mid = own + t
        sl = pl.ds(pl.multiple_of(zi * group, group), group)
        pm_ref[sl, :] = mid
        nh, nl = split(layer_norm(mid))
        pr = dot_nn(jnp.concatenate([nh, nl], 1), in_hh) + dot_nn(nh, in_l)
        redge_ref[sl, :] = sigmoid(pr[:, 3 * ch : 4 * ch]) * pr[:, 2 * ch : 3 * ch]
        for s in range(4):
            for k in range(I):
                at = pl.multiple_of(zi * group + (s * I + k) * I, I)
                rbuf[z, pl.ds(at, I), :] = redge_ref[
                    pl.ds(zi * group + s * 64 + k, I, stride=I), :
                ]
        for n in range(parts // zs):
            send_on(0, zi * (parts // zs) + n)
        lall[2 * y + core, sl, :] = sigmoid(pr[:, ch : 2 * ch]) * pr[:, :ch]
        l_copy(0, zi).start()
        l_copy(1, zi).start()
        gate_ref[sl, :] = sigmoid(pr[:, 4 * ch :])

    part = rows // parts

    def line_copy(source, h, send, target):
        at = rbuf.at[source, pl.ds(pl.multiple_of(h * part, part), part)]
        return pltpu.make_async_remote_copy(
            src_ref=at,
            dst_ref=at,
            send_sem=send,
            recv_sem=line_recv.at[source, h],
            device_id=(target, c),
            device_id_type=MESH,
        )

    def line_up(t, h):
        return line_copy(z - t, h, up_sem.at[t, h], up_row)

    def line_down(t, h):
        return line_copy(z + t, h, down_sem.at[t, h], down_row)

    def send_on(t, h):
        @pl.when(jnp.logical_and(z >= t, z < Z - 1))
        def _():
            line_up(t, h).start()

        @pl.when(jnp.logical_and(z + t < Z, z > 0))
        def _():
            line_down(t, h).start()

    own_l = 2 * y + core

    def l_copy(n, zi):
        slot = own_l if n < 2 else 2 * (1 - y) + core
        at = lall.at[slot, pl.ds(pl.multiple_of(zi * group, group), group)]
        return pltpu.make_async_remote_copy(
            src_ref=at,
            dst_ref=at,
            send_sem=l_send.at[n, zi],
            recv_sem=l_recv.at[slot, zi],
            device_id=(y_row if n == 1 else core_row, c),
            device_id_type=MESH,
        )

    def l_arrived(slot, zi):
        at = lall.at[slot, pl.ds(pl.multiple_of(zi * group, group), group)]
        pltpu.make_async_remote_copy(
            src_ref=at,
            dst_ref=at,
            send_sem=l_send.at[0, zi],
            recv_sem=l_recv.at[slot, zi],
            device_id=(core_row, c),
            device_id_type=MESH,
        ).wait_recv()

    def part_order(source, n):
        if zs == 1:
            return n
        return turned(n, source)

    def piece(d, source, q):
        dest_col = lax.div(source, zs)
        slot = lax.rem(source, zs) * 4 + own_l
        target = row_at(z, lax.rem(y + q // 2, 2), lax.rem(core + q, 2))
        return (
            dest_col,
            slot,
            pltpu.make_async_remote_copy(
                src_ref=mst.at[d, q],
                dst_ref=accb.at[c, slot],
                send_sem=m_send.at[d, q],
                recv_sem=m_recv.at[c, slot],
                device_id=(target, dest_col),
                device_id_type=MESH,
            ),
        )

    def triangle(d, source, h, first, last):
        for pair in ((2, 3), (1, 0)):
            who = [2 * lax.rem(y + q // 2, 2) + lax.rem(core + q, 2) for q in pair]

            def step(s, acc):
                acc = list(acc)
                s = h * (nr // parts) + s
                for k in range(I):
                    rv = rbuf[source, pl.ds(pl.multiple_of((s * I + k) * I, I), I), :]
                    for n in range(2):
                        for i in range(I):
                            lv = lall[who[n], pl.ds(s * 64 + i * I + k, 1), :]
                            acc[n * I + i] = acc[n * I + i] + lv * rv
                return tuple(acc)

            if first:
                acc = tuple(jnp.zeros((I, channels), f32) for _ in range(2 * I))
            else:
                acc = tuple(
                    mst[d, q, i * I : (i + 1) * I, :] for q in pair for i in range(I)
                )
            acc = lax.fori_loop(0, nr // parts, step, acc)
            for n, q in enumerate(pair):
                for i in range(I):
                    mst[d, q, i * I : (i + 1) * I, :] = acc[n * I + i]
                if not last:
                    continue
                dest_col, slot, copy = piece(d, source, q)
                if q:
                    copy.start()
                else:

                    @pl.when(dest_col == c)
                    def _():
                        accb[c, slot] = mst[d, q]

                    @pl.when(dest_col != c)
                    def _():
                        copy.start()

    def finish(source, exists):
        @pl.when(jnp.logical_and(exists, lax.div(source, zs) == c))
        def _():
            base = lax.rem(source, zs) * 4

            def arrived(k, s):
                pltpu.make_async_remote_copy(
                    src_ref=mst.at[0, 0],
                    dst_ref=accb.at[k, s],
                    send_sem=m_send.at[0, 0],
                    recv_sem=m_recv.at[k, s],
                    device_id=(core_row, c),
                    device_id_type=MESH,
                ).wait_recv()

            for n in range(1, 4):
                arrived(c, base + 2 * lax.rem(y + n // 2, 2) + lax.rem(core + n, 2))
            for n in range(1, C):
                for s in range(4):
                    arrived(lax.rem(c + n, C), base + s)
            for s in range(0, 4, 2):
                mixed = accb[0, pl.ds(base + s, 2)].reshape(128, channels)
                for k in range(1, C):
                    mixed = mixed + accb[k, pl.ds(base + s, 2)].reshape(128, channels)
                nh, nl = split(layer_norm(mixed))
                t = dot_nn(jnp.concatenate([nh, nl], 1), out_hh) + dot_nn(nh, out_l)
                sl = pl.ds(pl.multiple_of((base + s) * 64, 64), 128)
                t = pm_ref[sl, :] + gate_ref[sl, :] * t
                for n in range(2):
                    for i in range(I):
                        at = pl.multiple_of(i * J + (base + s + n) * I, I)
                        out_ref[pl.ds(at, I), :] = t[(n * I + i) * I : (n * I + i + 1) * I]

    outer_block(a_links(0)[0])
    for t in range(1, zs):
        a_line(t)
    a_across(0)
    for t in range(zs):
        zi = turned(t, z)
        if t > 0:
            outer_block(zi * 4 + y * 2 + core)
        outer_block(zi * 4 + (1 - y) * 2 + core)
        for yy in (y, 1 - y):
            slot = zi * 4 + yy * 2 + 1 - core
            for u in range(pieces):
                a_copy(slot, u, a_core.at[t, 1, u], core_row).wait_recv()
            outer_block(slot)
        if t + 1 < zs:
            a_across(t + 1)
        pair_group(zi)

    def pass_on(t, n):
        below = part_order(z - t, n)
        above = part_order(z + t, n)

        @pl.when(z >= t)
        def _():
            line_up(t, below).wait_recv()

            @pl.when(z < Z - 1)
            def _():
                line_up(t, below).start()

        @pl.when(z + t < Z)
        def _():
            line_down(t, above).wait_recv()

            @pl.when(z > 0)
            def _():
                line_down(t, above).start()

    def add_up(t, n):
        @pl.when(z >= t)
        def _():
            triangle(t, z - t, part_order(z - t, n), n == 0, n == parts - 1)

        @pl.when(z + t < Z)
        def _():
            triangle(Z - 1 + t, z + t, part_order(z + t, n), n == 0, n == parts - 1)

        if n == parts - 1:
            if t == 1:
                finish(z, z >= 0)
            else:
                finish(z - t + 1, z >= t - 1)
                finish(z + t - 1, z + t - 1 < Z)

    for n in range(parts):
        pass_on(1, n)
        if n < zs:
            zi = turned(n, z)
            l_arrived(2 * (1 - y) + core, zi)
            l_copy(2, zi).start()
    for t in range(zs):
        zi = turned(t, z)
        l_arrived(2 * y + 1 - core, zi)
        l_arrived(2 * (1 - y) + 1 - core, zi)
    for n in range(parts):
        triangle(0, z, part_order(z, n), n == 0, n == parts - 1)
    todo = [(1, n) for n in range(parts)]
    order = [(t, n) for t in range(2, Z) for n in range(parts)]
    for step in order[:-1]:
        add_up(*todo.pop(0))
        pass_on(*step)
        todo.append(step)
    for step in todo:
        add_up(*step)
    for step in order[-1:]:
        pass_on(*step)
        add_up(*step)
    finish(z - Z + 1, z >= Z - 1)
    finish(z + Z - 1, z < 1)

    for t in range(zs):
        slot, source, goes_up, goes_down = a_links(t)
        across = turned(t, z) * 4 + (1 - y) * 2 + core
        for u in range(pieces):

            @pl.when(goes_up)
            def _():
                a_copy(slot, u, a_up.at[t, u], up_row).wait_send()

            @pl.when(goes_down)
            def _():
                a_copy(slot, u, a_down.at[t, u], down_row).wait_send()

            a_copy(slot, u, a_y.at[t, u], y_row).wait_send()
            a_copy(slot, u, a_core.at[t, 0, u], core_row).wait_send()
            a_copy(across, u, a_core.at[t, 1, u], core_row).wait_send()
        for n in range(3):
            l_copy(n, t).wait_send()
    for t in range(Z):
        for h in range(parts):

            @pl.when(jnp.logical_and(z >= t, z < Z - 1))
            def _():
                line_up(t, h).wait_send()

            @pl.when(jnp.logical_and(z + t < Z, z > 0))
            def _():
                line_down(t, h).wait_send()

    def pieces_left(d, source):
        for q in range(4):
            dest_col, _, copy = piece(d, source, q)
            if q:
                copy.wait_send()
            else:

                @pl.when(dest_col != c)
                def _():
                    copy.wait_send()

    pieces_left(0, z)
    for t in range(1, Z):

        @pl.when(z >= t)
        def _():
            pieces_left(t, z - t)

        @pl.when(z + t < Z)
        def _():
            pieces_left(Z - 1 + t, z + t)


def per_device(R, C, msa, pair, first, second, outer_w, tri_in, gate_w, tri_out):
    S, I, depth = msa.shape
    J, channels = pair.shape[1:]
    half = first.shape[1]
    nr = R // C
    zs = nr // 4
    Z = R // 4
    rows = nr * I * I
    parts = max(2, zs)
    operands = (
        msa.reshape(S * I, depth),
        pair.reshape(I * J, channels),
        first.T,
        second.T,
        outer_w,
        tri_in,
        gate_w,
        tri_out,
    )
    dma = pltpu.SemaphoreType.DMA
    out = pl.pallas_call(
        functools.partial(kernel, (S, I, J, R, C, half, channels)),
        out_shape=jax.ShapeDtypeStruct((I * J, channels), f32),
        in_specs=[pl.BlockSpec(memory_space=pltpu.HBM)] * 8,
        out_specs=pl.BlockSpec(memory_space=pltpu.VMEM),
        scratch_shapes=[pltpu.VMEM(x.shape, f32) for x in operands]
        + [
            pltpu.VMEM((depth // 128, S * I, 128), f32),
            pltpu.VMEM((I * half, S), f32),
            pltpu.VMEM((I * half, S), f32),
            pltpu.VMEM((nr, half * I, S), f32),
            pltpu.VMEM((half * half, channels), f32),
            pltpu.VMEM((nr, I * I, half * half), f32),
            pltpu.VMEM((rows, channels), f32),
            pltpu.VMEM((rows, channels), f32),
            pltpu.VMEM((rows, channels), f32),
            pltpu.VMEM((4, rows, channels), f32),
            pltpu.VMEM((Z, rows, channels), f32),
            pltpu.VMEM((2 * Z - 1, 4, I * I, channels), f32),
            pltpu.VMEM((C, nr, I * I, channels), f32),
            dma((zs, pieces)),
            dma((zs, pieces)),
            dma((zs, pieces)),
            dma((zs, 2, pieces)),
            dma((nr, pieces)),
            dma((len(operands),)),
            dma((3, zs)),
            dma((4, zs)),
            dma((Z, parts)),
            dma((Z, parts)),
            dma((Z, parts)),
            dma((2 * Z - 1, 4)),
            dma((C, nr)),
        ],
        compiler_params=pltpu.CompilerParams(
            collective_id=0, has_side_effects=True, vmem_limit_bytes=62 * 1024 * 1024
        ),
        cost_estimate=pl.CostEstimate(
            flops=6 * 180 * 10**6, bytes_accessed=3 * 10**6, transcendentals=200000
        ),
    )(*operands)
    return out.reshape(I, J, channels)


def solution(mesh):
    placed = (P(None, "row", None), P("row", "col", None), P(), P(), P(), P(), P(), P())
    return jax.shard_map(
        functools.partial(per_device, mesh.shape["row"], mesh.shape["col"]),
        mesh=mesh,
        in_specs=placed,
        out_specs=P("row", "col", None),
        check_vma=False,
    )
```
